32 devices in a mesh: groups: 2 (over x), tile: 16 (over z, y, core).
Axes of the slice: x: 2, y: 2, z: 4, core: 2. Of those that a mesh axis runs over, the one named last changes fastest.
Arguments:
- start_model: float32 [2, 32768, 128], P(None, ('groups', 'tile')), parts along dimension 1, may hold values from -6 to 6
- v_basis: bfloat16 [2, 26624, 1024], P(None, ('groups', 'tile')), parts along dimension 1, may hold values from -0.125 to 0.125
- u_basis: bfloat16 [2, 1, 832, 32768], P(None, None, None, ('groups', 'tile')), parts along dimension 3, may hold values from -0.15625 to 0.15625
- records: bfloat16 [32, 128, 32768], P(None, None, ('groups', 'tile')), parts along dimension 2, may hold values from -6 to 6
- tile_ranks: int32 [2, 16, 16], P('groups'), parts along dimension 0, may hold values from 8 to 96, as said below
- window_start: int32 [128, 32768], P(None, ('groups', 'tile')), parts along dimension 1, may hold values from 0 to 7, as said below
- window_stop: int32 [128, 32768], P(None, ('groups', 'tile')), parts along dimension 1, may hold values from 16 to 31
Outputs:
- final_model: float32 [2, 32768, 128], P(None, ('groups', 'tile')), parts along dimension 1
The draws below stay inside these ranges and needn't reach their ends.
There are 2 independent parts, one for each index of `groups`. The reference program is written for one: setup_inputs(seed, part) draws one part's arguments, and reference() takes and returns one part's arrays. A program takes and returns all parts, laid end to end along the dimension named above; each array names one. Nothing has to cross between parts.
Inputs may be any that keep to these rules, and one draw needn't show every extreme that they name: `tile_ranks`: every tile row and every tile column of one frequency holds the same 16 ranks, each once, and they sum to 832; every frequency has tiles of rank 96 and of rank 8. window_stop - window_start lies between 16 and 24 for every pair.
All inputs are finite; a program needn't handle non-finite values.
Results may differ from the reference program's by a relative error of at most 0.012.
Values may be sent and summed in bfloat16 or wider, within the bound.
No kernel may reach another device: no remote copies, remote signals or barrier semaphores. Data moves between devices by JAX's collectives and lax.ppermute only.
A program may use at most 128 MiB of HBM per device.

```python
import math
import jax
import jax.numpy as jnp
from jax import lax

NB = 1024
CT = 16
RT = 16
NVS = 128
RMIN = 8
RMAX = 96
NT = 32
ITERS = 2
F = 1
N = 16384
NR = 16384
RSUM = 832
PIECES = 1
PROWS = 1024


def permute_tiles(subkey):
    return jax.random.permutation(subkey, CT).astype(jnp.int32)


def rank_layout(key):
    half_count = CT // 2
    chosen = jax.random.randint(jax.random.fold_in(key, 11), (F, half_count), RMIN, RMAX + 1)
    leading = jnp.arange(half_count, dtype=jnp.int32)[None, :] == 0
    chosen = jnp.where(leading, RMAX, chosen)
    rank_values = jnp.concatenate([chosen, RMIN + RMAX - chosen], axis=1)
    row_keys = jax.random.split(jax.random.fold_in(key, 12), F)
    col_keys = jax.random.split(jax.random.fold_in(key, 13), F)
    row_order = jax.vmap(permute_tiles)(row_keys)
    col_order = jax.vmap(permute_tiles)(col_keys)
    position = (row_order[:, :, None] + col_order[:, None, :]) % CT
    spread = jnp.broadcast_to(rank_values[:, None, :], (F, RT, CT))
    return jnp.take_along_axis(spread, position, axis=2).astype(jnp.int32)


def window_layout(key):
    openings = jax.random.randint(jax.random.fold_in(key, 21), (NVS, NR), 0, NT // 4)
    spans = jax.random.randint(jax.random.fold_in(key, 22), (NVS, NR), NT // 2, 3 * NT // 4 + 1)
    return (openings.astype(jnp.int32), (openings + spans).astype(jnp.int32))


def draw_tile_ranks(key, part):
    return rank_layout(key)


def draw_window_start(key, part):
    return window_layout(key)[0]


def draw_window_stop(key, part):
    return window_layout(key)[1]


def block_levels(stream_key, shape, pieces, low, top_value):
    level = 1.0
    for dim, parts in pieces:
        heights = jax.random.uniform(jax.random.fold_in(jax.random.fold_in(stream_key, 6), dim), (parts,), jnp.float32, low / len(pieces), top_value / len(pieces))
        level = level * jnp.repeat(jnp.exp(heights), shape[dim] // parts).reshape((-1,) + (1,) * (len(shape) - 1 - dim))
    return level


def scatter_about(stream_key, extent, scale, reach, cuts=(), kind=jnp.bfloat16):
    factor_of = block_levels(stream_key, extent, cuts, -0.22, 0.18) if cuts else 1.0
    values = jax.random.normal(stream_key, extent, jnp.float32) * scale * factor_of
    return jnp.minimum(jnp.maximum(values, -reach), reach).astype(kind)


def setup_inputs(seed: int = 0, part: int = 0) -> dict:
    streams_of = jax.random.split(jax.random.key(seed), 8)
    own_keys = jax.random.split(jax.random.fold_in(streams_of[7], part), 8)
    start_model = scatter_about(own_keys[0], (2, F * N, NVS), 1.0, 6.0, ((1, 16),), jnp.float32)
    v_basis = scatter_about(own_keys[1], (2, F * CT * RSUM, NB), (2 * NB) ** -0.5, 0.125, ((1, 16),))
    u_basis = scatter_about(own_keys[2], (2, F, RSUM, NR), (2 * RSUM) ** -0.5, 0.15625, ((3, 16),))
    records = scatter_about(own_keys[3], (NT, NVS, NR), 1.0, 6.0, ((2, 16),))
    tile_ranks = draw_tile_ranks(jax.random.fold_in(jax.random.fold_in(streams_of[7], part), 71), part)
    window_start = draw_window_start(jax.random.fold_in(jax.random.fold_in(streams_of[7], part), 71), part)
    window_stop = draw_window_stop(jax.random.fold_in(jax.random.fold_in(streams_of[7], part), 71), part)
    return dict(start_model=start_model, v_basis=v_basis, u_basis=u_basis, records=records, tile_ranks=tile_ranks, window_start=window_start, window_stop=window_stop)


step_size = 0.5
precise = lax.Precision.HIGHEST

def wave_tables(bin_count, sample_count):
    moments = jnp.arange(sample_count, dtype=jnp.float32)
    bin_ids = jnp.arange(bin_count, dtype=jnp.float32) + 1.0
    phases = 2.0 * math.pi / sample_count * bin_ids[:, None] * moments[None, :]
    factor = math.sqrt(2.0 / sample_count)
    return (jnp.cos(phases) * factor, jnp.sin(phases) * factor)

def unpack_index(starts, slot_total):
    slot_ids = jnp.arange(slot_total, dtype=jnp.int32)
    owners = lax.optimization_barrier(jnp.sum((starts[..., None, :] <= slot_ids[:, None]).astype(jnp.int32), axis=-1)) - 1
    owner_start = jnp.take_along_axis(starts, owners, axis=-1)
    return (owners, slot_ids - owner_start)

def piece_tree(partials, axis):
    current = partials
    while current.shape[axis] > 1:
        half_count = current.shape[axis] // 2
        lower_part = lax.slice_in_dim(current, 0, half_count, axis=axis).astype(jnp.float32)
        upper_part = lax.slice_in_dim(current, half_count, 2 * half_count, axis=axis).astype(jnp.float32)
        current = lax.optimization_barrier((lower_part + upper_part).astype(jnp.bfloat16))
    return jnp.squeeze(current, axis)

def reference(start_model, v_basis, u_basis, records, tile_ranks, window_start, window_stop):
    down_offsets = jnp.cumsum(tile_ranks, axis=1) - tile_ranks
    side_offsets = jnp.cumsum(tile_ranks, axis=2) - tile_ranks
    col_owner, col_slot = unpack_index(side_offsets, RSUM)
    gather_u = (col_owner * RSUM + jnp.take_along_axis(down_offsets, col_owner, axis=2) + col_slot).astype(jnp.int32)
    down_swap = jnp.transpose(down_offsets, (0, 2, 1))
    side_swap = jnp.transpose(side_offsets, (0, 2, 1))
    row_owner, row_slot = unpack_index(down_swap, RSUM)
    gather_v = (row_owner * RSUM + jnp.take_along_axis(side_swap, row_owner, axis=2) + row_slot).astype(jnp.int32)
    v_blocks = jnp.transpose(v_basis.reshape(2, F, CT, RSUM, NB), (1, 0, 2, 3, 4))
    u_blocks = jnp.transpose(u_basis, (1, 0, 2, 3))
    cos_table, sin_table = wave_tables(F, NT)

    def forward_one(operands):
        v_freq, x_freq, u_freq, gather_ids = operands
        v_wide = v_freq.astype(jnp.float32)
        coeff_real = jnp.einsum('jkn,jns->jks', v_wide[0], x_freq[0]) - jnp.einsum('jkn,jns->jks', v_wide[1], x_freq[1])
        coeff_imag = jnp.einsum('jkn,jns->jks', v_wide[0], x_freq[1]) + jnp.einsum('jkn,jns->jks', v_wide[1], x_freq[0])
        packed = lax.optimization_barrier(jnp.stack([coeff_real, coeff_imag]).astype(jnp.bfloat16))
        packed = packed.astype(jnp.float32).reshape(2, CT * RSUM, NVS)
        chosen = packed[:, gather_ids]
        u_wide = u_freq.astype(jnp.float32).reshape(2, RSUM, RT, NB)
        pred_real = jnp.einsum('iks,kin->sin', chosen[0], u_wide[0]) - jnp.einsum('iks,kin->sin', chosen[1], u_wide[1])
        pred_imag = jnp.einsum('iks,kin->sin', chosen[0], u_wide[1]) + jnp.einsum('iks,kin->sin', chosen[1], u_wide[0])
        return jnp.stack([pred_real, pred_imag]).reshape(2, NVS, NR)

    def misfit_block(operands):
        pred_block, record_block, open_block, close_block = operands
        traces = jnp.einsum('ft,fsn->tsn', cos_table, pred_block[:, 0], precision=precise) - jnp.einsum('ft,fsn->tsn', sin_table, pred_block[:, 1], precision=precise)
        moments = jnp.arange(NT, dtype=jnp.int32)[:, None, None]
        inside = (moments >= open_block[None]) & (moments < close_block[None])
        residual = jnp.where(inside, traces - record_block.astype(jnp.float32), jnp.zeros((), jnp.float32))
        back_real = jnp.einsum('ft,tsn->fsn', cos_table, residual, precision=precise)
        back_imag = -jnp.einsum('ft,tsn->fsn', sin_table, residual, precision=precise)
        return jnp.stack([back_real, back_imag], axis=1).astype(jnp.bfloat16)

    def adjoint_one(operands):
        u_freq, back_freq, v_freq, gather_ids = operands
        u_wide = u_freq.astype(jnp.float32).reshape(2, RSUM, RT, PIECES, PROWS)
        back_wide = back_freq.astype(jnp.float32).reshape(2, NVS, RT, PIECES, PROWS)
        part_real = jnp.einsum('kipn,sipn->ipks', u_wide[0], back_wide[0]) + jnp.einsum('kipn,sipn->ipks', u_wide[1], back_wide[1])
        part_imag = jnp.einsum('kipn,sipn->ipks', u_wide[0], back_wide[1]) - jnp.einsum('kipn,sipn->ipks', u_wide[1], back_wide[0])
        partials = lax.optimization_barrier(jnp.stack([part_real, part_imag]).astype(jnp.bfloat16))
        summed = piece_tree(partials, 2)
        summed = summed.astype(jnp.float32).reshape(2, RT * RSUM, NVS)
        chosen = summed[:, gather_ids]
        v_wide = v_freq.astype(jnp.float32)
        grad_real = jnp.einsum('jkn,jks->jns', v_wide[0], chosen[0]) + jnp.einsum('jkn,jks->jns', v_wide[1], chosen[1])
        grad_imag = jnp.einsum('jkn,jks->jns', v_wide[0], chosen[1]) - jnp.einsum('jkn,jks->jns', v_wide[1], chosen[0])
        return jnp.stack([grad_real, grad_imag])
    record_blocks = jnp.transpose(records.reshape(NT, NVS, RT, NB), (2, 0, 1, 3))
    open_blocks = jnp.transpose(window_start.reshape(NVS, RT, NB), (1, 0, 2))
    close_blocks = jnp.transpose(window_stop.reshape(NVS, RT, NB), (1, 0, 2))
    current = start_model
    for iteration in range(ITERS):
        rounded = lax.optimization_barrier(current.astype(jnp.bfloat16)).astype(jnp.float32)
        x_blocks = jnp.transpose(rounded.reshape(2, F, CT, NB, NVS), (1, 0, 2, 3, 4))
        predicted = lax.map(forward_one, (v_blocks, x_blocks, u_blocks, gather_u))
        pred_blocks = jnp.transpose(predicted.reshape(F, 2, NVS, RT, NB), (3, 0, 1, 2, 4))
        back_blocks = lax.map(misfit_block, (pred_blocks, record_blocks, open_blocks, close_blocks))
        backward = jnp.transpose(back_blocks, (1, 2, 3, 0, 4)).reshape(F, 2, NVS, NR)
        gradient = lax.map(adjoint_one, (u_blocks, backward, v_blocks, gather_v))
        gradient = jnp.transpose(gradient, (1, 0, 2, 3, 4)).reshape(2, F * N, NVS)
        current = current - step_size * gradient
    return current
```

```python
import functools
import math

import jax
import jax.numpy as jnp
import numpy as np
from jax import lax
from jax.experimental import pallas as pl
from jax.experimental.pallas import tpu as pltpu
from jax.sharding import PartitionSpec as P

RMAX = 96
ITERS = 2
STEP = 0.5
START_MAX = 7
STOP_MIN = 16
STOP_MAX = 31
F32 = jnp.float32
BF16 = jnp.bfloat16

SMEM = pl.BlockSpec(memory_space=pltpu.SMEM)
VMEM = pl.BlockSpec(memory_space=pltpu.VMEM)
PARAMS = pltpu.CompilerParams(vmem_limit_bytes=12 * 1024 * 1024)


def phase_rows(freq_count, sample_count):
    moments = np.arange(sample_count, dtype=np.float64)
    bins = np.arange(freq_count, dtype=np.float64) + 1.0
    phases = 2.0 * math.pi / sample_count * bins[:, None] * moments[None, :]
    factor = math.sqrt(2.0 / sample_count)
    rows = np.stack([np.cos(phases), -np.sin(phases)], axis=1) * factor
    return rows.reshape(2 * freq_count, sample_count).astype(np.float32)


def pair_list(count):
    return [(a, b) for a in range(count) for b in range(a, count)]


def side_by_side(real, imag):
    return jnp.concatenate([real, imag], axis=1).astype(BF16)


def dot(left, right):
    return jnp.dot(left, right, preferred_element_type=F32)


def dot_last(left, right):
    return lax.dot_general(left, right, (((1,), (1,)), ((), ())), preferred_element_type=F32)


def above(upper, lower):
    return jnp.concatenate([upper, lower], axis=0).astype(BF16)


def rows_turned(rows_ref, rank_total):
    return rows_ref[0, :rank_total, :].T, rows_ref[1, :rank_total, :].T


def store_slots(ranks_of, rows_ref, slots_ref, slot_count, repeat, first_slot):
    start = 0
    for k in range(slot_count):
        block = jnp.concatenate([rows_ref[c, pl.ds(start, RMAX), :] for c in range(2)], axis=1)
        block = block.astype(BF16)
        for p in range(repeat):
            slots_ref[first_slot + k * repeat + p] = block
        start = start + ranks_of(k)


def piece_tree(blocks):
    while len(blocks) > 1:
        half = len(blocks) // 2
        blocks = [
            (blocks[q].astype(F32) + blocks[q + half].astype(F32)).astype(BF16)
            for q in range(half)
        ]
    return blocks[0]


def load_slots(ranks_of, slots_ref, rows_ref, slot_count, repeat, first_slot):
    start = 0
    lanes = rows_ref.shape[2]
    for k in range(slot_count):
        block = piece_tree([slots_ref[first_slot + k * repeat + p] for p in range(repeat)])
        block = block.astype(F32)
        for c in range(2):
            rows_ref[c, pl.ds(start, RMAX), :] = block[:, c * lanes : (c + 1) * lanes]
        start = start + ranks_of(k)


def clear_tail(rows_ref, rank_total):
    tail = (2, rows_ref.shape[1] - rank_total, rows_ref.shape[2])
    rows_ref[:, rank_total:, :] = jnp.zeros(tail, F32)


def store_rows(rows_ref, rank_total, value):
    lanes = rows_ref.shape[2]
    for c in range(2):
        rows_ref[c, :rank_total, :] = value[:, c * lanes : (c + 1) * lanes]


def column_of(ranks_ref):
    cols = ranks_ref.shape[2]
    device = lax.axis_index("tile")
    freq, col = device // cols, device % cols
    return lambda i: ranks_ref[freq, i, col]


def project(v_ref, real, imag, rows_ref):
    rank_total = v_ref.shape[1]
    value = dot(v_ref[0], side_by_side(real, imag)) + dot(v_ref[1], side_by_side(-imag, real))
    store_rows(rows_ref, rank_total, value)


def first_kernel(pieces, ranks_ref, v_ref, x_ref, slots_ref, rows_ref):
    clear_tail(rows_ref, v_ref.shape[1])
    project(v_ref, x_ref[0], x_ref[1], rows_ref)
    store_slots(column_of(ranks_ref), rows_ref, slots_ref, ranks_ref.shape[1], pieces, 0)


def misfit_kernel(
    pieces, ranks_ref, in_ref, u_ref, gram_ref, data_ref, out_ref, rows_ref, pred_ref, field_ref
):
    freqs, _, cols = ranks_ref.shape
    rank_total, width = u_ref.shape[2:]
    lanes = in_ref.shape[2] // 2
    row = lax.axis_index("tile") // pieces
    for f in range(freqs):
        ranks_of = lambda j, f=f: ranks_ref[f, row, j]
        load_slots(ranks_of, in_ref, rows_ref, cols, 1, f * cols)
        real, imag = rows_turned(rows_ref, rank_total)
        pred_ref[f] = dot(above(real, imag), u_ref[0, f]) + dot(above(-imag, real), u_ref[1, f])
    parts = 2 * freqs
    where = {pair: k for k, pair in enumerate(pair_list(parts))}
    clear_tail(rows_ref, rank_total)
    for a in range(parts):
        total = -data_ref[a]
        for b in range(parts):
            half = pred_ref[b // 2, b % 2 * lanes : (b % 2 + 1) * lanes, :]
            total = total + gram_ref[where[(min(a, b), max(a, b))]] * half
        field_ref[a] = total.astype(BF16)
    for f in range(freqs):
        ranks_of = lambda j, f=f: ranks_ref[f, row, j]
        real, imag = field_ref[2 * f], field_ref[2 * f + 1]
        value = dot_last(u_ref[0, f], above(real, imag)) + dot_last(
            u_ref[1, f], above(imag, -real)
        )
        store_rows(rows_ref, rank_total, value)
        store_slots(ranks_of, rows_ref, out_ref, cols, 1, f * cols)


def update_kernel(pieces, last, ranks_ref, in_ref, v_ref, x_ref, *rest):
    if last:
        new_ref, rows_ref = rest
    else:
        new_ref, slots_ref, rows_ref = rest
    rank_total = v_ref.shape[1]
    lanes = in_ref.shape[2] // 2
    ranks_of = column_of(ranks_ref)
    load_slots(ranks_of, in_ref, rows_ref, ranks_ref.shape[1], pieces, 0)
    real, imag = rows_turned(rows_ref, rank_total)
    gradient = dot(above(real, imag), v_ref[0]) + dot(above(imag, -real), v_ref[1])
    new_ref[0] = x_ref[0] - STEP * gradient[:lanes].T
    new_ref[1] = x_ref[1] - STEP * gradient[lanes:].T
    if not last:
        clear_tail(rows_ref, rank_total)
        project(v_ref, new_ref[0], new_ref[1], rows_ref)
        store_slots(ranks_of, rows_ref, slots_ref, ranks_ref.shape[1], pieces, 0)


def harmonic_sums(freq_count, sample_count):
    multiples = np.arange(2 * freq_count + 1, dtype=np.float64)[:, None]
    phases = 2.0 * math.pi / sample_count * multiples * np.arange(sample_count)[None, :]
    waves = np.stack([np.cos(phases), np.sin(phases)]) / sample_count
    sums = np.concatenate([np.zeros((2, waves.shape[1], 1)), np.cumsum(waves, axis=2)], axis=2)
    return sums.astype(np.float32)


def gram_parts(a, b):
    f, g = a // 2 + 1, b // 2 + 1
    apart, lean = abs(f - g), 1.0 if f > g else -1.0 if f < g else 0.0
    if a % 2 == 0 and b % 2 == 0:
        return [(0, apart, 1.0), (0, f + g, 1.0)]
    if a % 2 == 1 and b % 2 == 1:
        return [(0, apart, 1.0), (0, f + g, -1.0)]
    if a % 2 == 0:
        return [(1, apart, lean), (1, f + g, -1.0)]
    return [(1, apart, -lean), (1, f + g, -1.0)]


def normal_kernel(phases, start_ref, stop_ref, records_ref, gram_ref, data_ref):
    parts, samples = phases.shape
    half = samples // 2
    pairs = pair_list(parts)
    sums = harmonic_sums(parts // 2, samples)
    terms = [[term for term in gram_parts(a, b) if term[2] != 0.0] for a, b in pairs]
    needed = sorted({(kind, k) for some in terms for kind, k, _ in some if (kind, k) != (1, 0)})
    chunk = 16

    def pick(level, table, first, last):
        value = jnp.full(level.shape, float(table[first]), F32)
        for t in range(first + 1, last + 1):
            value = jnp.where(level >= t, float(table[t]), value)
        return value

    def add_up(step, carry):
        rows = pl.ds(pl.multiple_of(step * chunk, chunk), chunk)
        begin, end = start_ref[rows, :], stop_ref[rows, :]
        waves = {}
        for kind, k in needed:
            if (kind, k) == (0, 0):
                waves[kind, k] = (end - begin).astype(F32) * (1.0 / samples)
            else:
                table = sums[kind, k]
                waves[kind, k] = pick(end, table, STOP_MIN, STOP_MAX) - pick(
                    begin, table, 0, START_MAX
                )
        for n, some in enumerate(terms):
            total = None
            for kind, k, sign in some:
                if (kind, k) == (1, 0):
                    continue
                if total is None:
                    total = waves[kind, k] if sign > 0 else -waves[kind, k]
                else:
                    total = total + waves[kind, k] if sign > 0 else total - waves[kind, k]
            gram_ref[n, rows, :] = total

        def seen(t):
            value = records_ref[t, rows, :].astype(F32)
            if t < START_MAX:
                value = jnp.where(begin <= t, value, 0.0)
            if t >= STOP_MIN:
                value = jnp.where(end > t, value, 0.0)
            return value

        for odd in (0, 1):
            some = [a for a in range(parts) if (a // 2 + 1) % 2 == odd]
            datas = [jnp.zeros(begin.shape, F32) for _ in some]
            for t in range(half if some else 0):
                late, early = t + half, seen(t)
                if late < STOP_MAX:
                    early = early - seen(late) if odd else early + seen(late)
                for k, a in enumerate(some):
                    datas[k] = datas[k] + float(phases[a, t]) * early
            for k, a in enumerate(some):
                data_ref[a, rows, :] = datas[k]
        return carry

    lax.fori_loop(0, start_ref.shape[0] // chunk, add_up, 0)


def normal_terms(phases, window_start, window_stop, records):
    samples, lanes, width = records.shape
    parts = phases.shape[0]
    pair_count = len(pair_list(parts))
    block = 128
    return pl.pallas_call(
        functools.partial(normal_kernel, phases),
        grid=(width // block,),
        in_specs=[
            pl.BlockSpec((lanes, block), lambda n: (0, n)),
            pl.BlockSpec((lanes, block), lambda n: (0, n)),
            pl.BlockSpec((samples, lanes, block), lambda n: (0, 0, n)),
        ],
        out_specs=[
            pl.BlockSpec((pair_count, lanes, block), lambda n: (0, 0, n)),
            pl.BlockSpec((parts, lanes, block), lambda n: (0, 0, n)),
        ],
        out_shape=[
            jax.ShapeDtypeStruct((pair_count, lanes, width), F32),
            jax.ShapeDtypeStruct((parts, lanes, width), F32),
        ],
        cost_estimate=pl.CostEstimate(
            flops=16 * records.size, bytes_accessed=3 * records.size, transcendentals=0
        ),
        compiler_params=PARAMS,
        name="normal_terms",
    )(window_start, window_stop, records)


def on_device(start_model, v_basis, u_basis, records, tile_ranks, window_start, window_stop):
    tiles = lax.axis_size("tile")
    freqs, rows, cols = tile_ranks.shape
    pieces = tiles // rows
    rank_total = v_basis.shape[1]
    lanes = start_model.shape[2]
    receivers = u_basis.shape[3]
    phases = phase_rows(freqs, records.shape[0])

    slots = jax.ShapeDtypeStruct((tiles, RMAX, 2 * lanes), BF16)
    model = jax.ShapeDtypeStruct(start_model.shape, F32)
    padded_rows = pltpu.VMEM((2, rank_total + RMAX, lanes), F32)
    exchange = lambda x: lax.all_to_all(x, "tile", split_axis=0, concat_axis=0, tiled=True)

    outgoing = pl.pallas_call(
        functools.partial(first_kernel, pieces),
        in_specs=[SMEM, VMEM, VMEM],
        out_specs=VMEM,
        out_shape=slots,
        scratch_shapes=[padded_rows],
        compiler_params=PARAMS,
        name="first_projection",
    )(tile_ranks, v_basis, start_model)
    gram, data = normal_terms(phases, window_start, window_stop, records)
    current = start_model
    for iteration in range(ITERS):
        arrived = exchange(outgoing)
        outgoing = pl.pallas_call(
            functools.partial(misfit_kernel, pieces),
            in_specs=[SMEM] + [VMEM] * 4,
            out_specs=VMEM,
            out_shape=slots,
            scratch_shapes=[
                padded_rows,
                pltpu.VMEM((freqs, 2 * lanes, receivers), F32),
                pltpu.VMEM((2 * freqs, lanes, receivers), BF16),
            ],
            compiler_params=PARAMS,
            name="misfit",
        )(tile_ranks, arrived, u_basis, gram, data)
        arrived = exchange(outgoing)
        last = iteration == ITERS - 1
        result = pl.pallas_call(
            functools.partial(update_kernel, pieces, last),
            in_specs=[SMEM] + [VMEM] * 3,
            out_specs=VMEM if last else [VMEM, VMEM],
            out_shape=model if last else [model, slots],
            scratch_shapes=[padded_rows],
            compiler_params=PARAMS,
            name="last_update" if last else "update",
        )(tile_ranks, arrived, v_basis, current)
        if last:
            current = result
        else:
            current, outgoing = result
    return current


def solution(mesh):
    in_specs = (
        P(None, ("groups", "tile"), None),
        P(None, ("groups", "tile"), None),
        P(None, None, None, ("groups", "tile")),
        P(None, None, ("groups", "tile")),
        P("groups", None, None),
        P(None, ("groups", "tile")),
        P(None, ("groups", "tile")),
    )
    out_specs = P(None, ("groups", "tile"), None)
    return jax.shard_map(
        on_device, mesh=mesh, in_specs=in_specs, out_specs=out_specs, check_vma=False
    )
```

```python
import functools
import math

import jax
import jax.numpy as jnp
import numpy as np
from jax import lax
from jax.experimental import pallas as pl
from jax.experimental.pallas import tpu as pltpu
from jax.sharding import PartitionSpec as P

RMAX = 96
ITERS = 2
STEP = 0.5
START_MAX = 7
STOP_MIN = 16
STOP_MAX = 31
F32 = jnp.float32
BF16 = jnp.bfloat16

SMEM = pl.BlockSpec(memory_space=pltpu.SMEM)
VMEM = pl.BlockSpec(memory_space=pltpu.VMEM)
HBM = pl.BlockSpec(memory_space=pltpu.HBM)
MIB = 1024 * 1024


def mebibytes(*arrays):
    return sum(-(-x.size * x.dtype.itemsize // MIB) for x in arrays)


def params(mib):
    return pltpu.CompilerParams(vmem_limit_bytes=mib * MIB)


def phase_rows(freq_count, sample_count):
    moments = np.arange(sample_count, dtype=np.float64)
    bins = np.arange(freq_count, dtype=np.float64) + 1.0
    phases = 2.0 * math.pi / sample_count * bins[:, None] * moments[None, :]
    factor = math.sqrt(2.0 / sample_count)
    rows = np.stack([np.cos(phases), -np.sin(phases)], axis=1) * factor
    return rows.reshape(2 * freq_count, sample_count).astype(np.float32)


def pair_list(count):
    return [(a, b) for a in range(count) for b in range(a, count)]


def side_by_side(real, imag):
    return jnp.concatenate([real, imag], axis=1).astype(BF16)


def dot(left, right):
    return jnp.dot(left, right, preferred_element_type=F32)


def dot_last(left, right):
    return lax.dot_general(left, right, (((1,), (1,)), ((), ())), preferred_element_type=F32)


def above(upper, lower):
    return jnp.concatenate([upper, lower], axis=0).astype(BF16)


def store_slots(ranks_of, rows_ref, slots_ref, slot_count, repeat, first_slot, done=None):
    start = 0
    for k in range(slot_count):
        block = jnp.concatenate([rows_ref[c, pl.ds(start, RMAX), :] for c in range(2)], axis=1)
        block = block.astype(BF16)
        for p in range(repeat):
            slots_ref[first_slot + k * repeat + p] = block
            if done is not None:
                done(first_slot + k * repeat + p)
        start = start + ranks_of(k)


def piece_tree(blocks):
    while len(blocks) > 1:
        half = len(blocks) // 2
        blocks = [
            (blocks[q].astype(F32) + blocks[q + half].astype(F32)).astype(BF16)
            for q in range(half)
        ]
    return blocks[0]


def load_slots(ranks_of, slots_ref, rows_ref, slot_count, repeat, first_slot):
    start = 0
    lanes = rows_ref.shape[2]
    for k in range(slot_count):
        block = piece_tree([slots_ref[first_slot + k * repeat + p] for p in range(repeat)])
        block = block.astype(F32)
        for c in range(2):
            rows_ref[c, pl.ds(start, RMAX), :] = block[:, c * lanes : (c + 1) * lanes]
        start = start + ranks_of(k)


def clear_tail(rows_ref, rank_total):
    tail = (2, rows_ref.shape[1] - rank_total, rows_ref.shape[2])
    rows_ref[:, rank_total:, :] = jnp.zeros(tail, F32)


def store_rows(rows_ref, rank_total, value):
    lanes = rows_ref.shape[2]
    for c in range(2):
        rows_ref[c, :rank_total, :] = value[:, c * lanes : (c + 1) * lanes]


def column_of(ranks_ref):
    cols = ranks_ref.shape[2]
    device = lax.axis_index("tile")
    freq, col = device // cols, device % cols
    return lambda i: ranks_ref[freq, i, col]


def turned_stack(real, imag):
    return jnp.concatenate([side_by_side(*real), side_by_side(*imag)], axis=0).T


def chunks(width):
    size = math.gcd(width, 256)
    return [pl.ds(k, size) for k in range(0, width, size)]


def flat(block):
    return block.reshape(block.shape[0] * block.shape[1], block.shape[2])


def project(v_ref, waves_ref, rows_ref):
    value = dot(v_ref[0], waves_ref[0]) + dot(v_ref[1], waves_ref[1])
    store_rows(rows_ref, v_ref.shape[1], value)


def first_kernel(
    pieces,
    ranks_hbm,
    v_hbm,
    x_hbm,
    slots_hbm,
    ranks_ref,
    v_ref,
    x_ref,
    waves_ref,
    rows_ref,
    slots_ref,
    in_sems,
    out_sems,
):
    pairs = [(x_hbm, x_ref), (v_hbm, v_ref), (ranks_hbm, ranks_ref)]
    copies = [pltpu.make_async_copy(*pair, in_sems.at[n]) for n, pair in enumerate(pairs)]
    for copy in copies:
        copy.start()
    clear_tail(rows_ref, v_ref.shape[1])
    copies[0].wait()
    real, imag = x_ref[0], x_ref[1]
    waves_ref[0] = side_by_side(real, imag)
    waves_ref[1] = side_by_side(-imag, real)
    copies[1].wait()
    copies[2].wait()
    project(v_ref, waves_ref, rows_ref)
    sent = []

    def send(last_slot):
        group = slots_ref.shape[0] // out_sems.shape[0]
        if last_slot % group == group - 1:
            these = pl.ds(last_slot - group + 1, group)
            sem = out_sems.at[last_slot // group]
            sent.append(pltpu.make_async_copy(slots_ref.at[these], slots_hbm.at[these], sem))
            sent[-1].start()

    ranks_of = column_of(ranks_ref)
    store_slots(ranks_of, rows_ref, slots_ref, ranks_ref.shape[1], pieces, 0, send)
    for copy in sent:
        copy.wait()


def misfit_kernel(
    pieces,
    cold,
    ranks_ref,
    in_ref,
    u_ref,
    gram_ref,
    data_ref,
    *rest,
):
    freqs, _, cols = ranks_ref.shape
    rank_total, width = u_ref.shape[2:]
    if cold:
        slots_hbm, gram_hbm, data_hbm = in_ref, gram_ref, data_ref
        out_ref, rows_ref, left_ref, field_ref, *fetch = rest
        in_ref, gram_ref, data_ref, pred_ref, sems = fetch
        pairs = [(slots_hbm, in_ref), (gram_hbm, gram_ref), (data_hbm, data_ref)]
        copies = [pltpu.make_async_copy(*pair, sems.at[n]) for n, pair in enumerate(pairs)]
        for copy in copies:
            copy.start()
        copies[0].wait()
    else:
        out_ref, rows_ref, left_ref, field_ref = rest
    lanes = in_ref.shape[2] // 2
    row = lax.axis_index("tile") // pieces
    for f in range(freqs):
        ranks_of = lambda j, f=f: ranks_ref[f, row, j]
        load_slots(ranks_of, in_ref, rows_ref, cols, 1, f * cols)
        real, imag = rows_ref[0, :rank_total, :], rows_ref[1, :rank_total, :]
        left_ref[f] = turned_stack((real, imag), (-imag, real))
    parts = 2 * freqs
    where = {pair: k for k, pair in enumerate(pair_list(parts))}
    clear_tail(rows_ref, rank_total)
    if cold:
        for f in range(freqs):
            pred_ref[f] = dot(left_ref[f], flat(u_ref[:, f]))
        copies[1].wait()
        copies[2].wait()
    for some in chunks(width):
        preds = []
        for f in range(freqs):
            if cold:
                pred = pred_ref[f, :, some]
            else:
                pred = dot(left_ref[f], flat(u_ref[:, f, :, some]))
            preds += [pred[:lanes], pred[lanes:]]
        fields = []
        for a in range(parts):
            total = -data_ref[a, :, some]
            for b in range(parts):
                total = total + gram_ref[where[min(a, b), max(a, b)], :, some] * preds[b]
            fields.append(total)
        for f in range(freqs):
            real, imag = fields[2 * f], fields[2 * f + 1]
            field_ref[f, 0, :, some] = above(real, imag)
            field_ref[f, 1, :, some] = above(imag, -real)
    for f in range(freqs):
        ranks_of = lambda j, f=f: ranks_ref[f, row, j]
        value = dot_last(u_ref[0, f], field_ref[f, 0]) + dot_last(u_ref[1, f], field_ref[f, 1])
        store_rows(rows_ref, rank_total, value)
        store_slots(ranks_of, rows_ref, out_ref, cols, 1, f * cols)


def update_kernel(pieces, last, ranks_ref, in_ref, v_ref, x_ref, *rest):
    if last:
        new_hbm, rows_ref, left_ref, new_ref, sems = rest
    else:
        new_ref, slots_ref, rows_ref, left_ref, waves_ref = rest
    rank_total, points = v_ref.shape[1:]
    lanes = in_ref.shape[2] // 2
    ranks_of = column_of(ranks_ref)
    load_slots(ranks_of, in_ref, rows_ref, ranks_ref.shape[1], pieces, 0)
    real, imag = rows_ref[0, :rank_total, :], rows_ref[1, :rank_total, :]
    left_ref[...] = turned_stack((real, imag), (imag, -real))
    copies = []
    for k, some in enumerate(chunks(points)):
        gradient = dot(left_ref[...], flat(v_ref[:, :, some]))
        real = x_ref[0, some, :] - STEP * gradient[:lanes].T
        imag = x_ref[1, some, :] - STEP * gradient[lanes:].T
        new_ref[0, some, :] = real
        new_ref[1, some, :] = imag
        if last:
            copies.append(
                pltpu.make_async_copy(new_ref.at[:, some, :], new_hbm.at[:, some, :], sems.at[k])
            )
            copies[k].start()
        else:
            waves_ref[0, some, :] = side_by_side(real, imag)
            waves_ref[1, some, :] = side_by_side(-imag, real)
    if last:
        for copy in copies:
            copy.wait()
    else:
        clear_tail(rows_ref, rank_total)
        project(v_ref, waves_ref, rows_ref)
        store_slots(ranks_of, rows_ref, slots_ref, ranks_ref.shape[1], pieces, 0)


def harmonic_sums(freq_count, sample_count):
    multiples = np.arange(2 * freq_count + 1, dtype=np.float64)[:, None]
    phases = 2.0 * math.pi / sample_count * multiples * np.arange(sample_count)[None, :]
    waves = np.stack([np.cos(phases), np.sin(phases)]) / sample_count
    sums = np.concatenate([np.zeros((2, waves.shape[1], 1)), np.cumsum(waves, axis=2)], axis=2)
    return sums.astype(np.float32)


def gram_parts(a, b):
    f, g = a // 2 + 1, b // 2 + 1
    apart, lean = abs(f - g), 1.0 if f > g else -1.0 if f < g else 0.0
    if a % 2 == 0 and b % 2 == 0:
        return [(0, apart, 1.0), (0, f + g, 1.0)]
    if a % 2 == 1 and b % 2 == 1:
        return [(0, apart, 1.0), (0, f + g, -1.0)]
    if a % 2 == 0:
        return [(1, apart, lean), (1, f + g, -1.0)]
    return [(1, apart, -lean), (1, f + g, -1.0)]


def normal_kernel(phases, start_ref, stop_ref, records_ref, gram_ref, data_ref):
    parts, samples = phases.shape
    half = samples // 2
    pairs = pair_list(parts)
    sums = harmonic_sums(parts // 2, samples)
    terms = [[term for term in gram_parts(a, b) if term[2] != 0.0] for a, b in pairs]
    needed = sorted({(kind, k) for some in terms for kind, k, _ in some if (kind, k) != (1, 0)})
    chunk = 16

    def pick(level, table, first, last):
        value = jnp.full(level.shape, float(table[first]), F32)
        for t in range(first + 1, last + 1):
            value = jnp.where(level >= t, float(table[t]), value)
        return value

    def add_up(step, carry):
        rows = pl.ds(pl.multiple_of(step * chunk, chunk), chunk)
        begin, end = start_ref[rows, :], stop_ref[rows, :]
        waves = {}
        for kind, k in needed:
            if (kind, k) == (0, 0):
                waves[kind, k] = (end - begin).astype(F32) * (1.0 / samples)
            else:
                table = sums[kind, k]
                waves[kind, k] = pick(end, table, STOP_MIN, STOP_MAX) - pick(
                    begin, table, 0, START_MAX
                )
        for n, some in enumerate(terms):
            total = None
            for kind, k, sign in some:
                if (kind, k) == (1, 0):
                    continue
                if total is None:
                    total = waves[kind, k] if sign > 0 else -waves[kind, k]
                else:
                    total = total + waves[kind, k] if sign > 0 else total - waves[kind, k]
            gram_ref[n, rows, :] = total

        def seen(t):
            value = records_ref[t, rows, :].astype(F32)
            if t < START_MAX:
                value = jnp.where(begin <= t, value, 0.0)
            if t >= STOP_MIN:
                value = jnp.where(end > t, value, 0.0)
            return value

        for odd in (0, 1):
            some = [a for a in range(parts) if (a // 2 + 1) % 2 == odd]
            datas = [jnp.zeros(begin.shape, F32) for _ in some]
            for t in range(half if some else 0):
                late, early = t + half, seen(t)
                if late < STOP_MAX:
                    early = early - seen(late) if odd else early + seen(late)
                for k, a in enumerate(some):
                    datas[k] = datas[k] + float(phases[a, t]) * early
            for k, a in enumerate(some):
                data_ref[a, rows, :] = datas[k]
        return carry

    lax.fori_loop(0, start_ref.shape[0] // chunk, add_up, 0)


def normal_terms(phases, window_start, window_stop, records):
    samples, lanes, width = records.shape
    parts = phases.shape[0]
    pair_count = len(pair_list(parts))
    block = 128
    return pl.pallas_call(
        functools.partial(normal_kernel, phases),
        grid=(width // block,),
        in_specs=[
            pl.BlockSpec((lanes, block), lambda n: (0, n)),
            pl.BlockSpec((lanes, block), lambda n: (0, n)),
            pl.BlockSpec((samples, lanes, block), lambda n: (0, 0, n)),
        ],
        out_specs=[
            pl.BlockSpec((pair_count, lanes, block), lambda n: (0, 0, n)),
            pl.BlockSpec((parts, lanes, block), lambda n: (0, 0, n)),
        ],
        out_shape=[
            jax.ShapeDtypeStruct((pair_count, lanes, width), F32),
            jax.ShapeDtypeStruct((parts, lanes, width), F32),
        ],
        cost_estimate=pl.CostEstimate(
            flops=16 * records.size, bytes_accessed=3 * records.size, transcendentals=0
        ),
        compiler_params=params(60),
        name="normal_terms",
    )(window_start, window_stop, records)


def on_device(start_model, v_basis, u_basis, records, tile_ranks, window_start, window_stop):
    tiles = lax.axis_size("tile")
    freqs, rows, cols = tile_ranks.shape
    pieces = tiles // rows
    rank_total = v_basis.shape[1]
    points, lanes = start_model.shape[1:]
    receivers = u_basis.shape[3]
    phases = phase_rows(freqs, records.shape[0])

    slots = jax.ShapeDtypeStruct((tiles, RMAX, 2 * lanes), BF16)
    model = jax.ShapeDtypeStruct(start_model.shape, F32)
    padded_rows = pltpu.VMEM((2, rank_total + RMAX, lanes), F32)
    waves = pltpu.VMEM((2, points, 2 * lanes), BF16)
    left = pltpu.VMEM((2 * lanes, 2 * rank_total), BF16)
    exchange = lambda x: lax.all_to_all(x, "tile", split_axis=0, concat_axis=0, tiled=True)

    outgoing = pl.pallas_call(
        functools.partial(first_kernel, pieces),
        in_specs=[HBM, HBM, HBM],
        out_specs=HBM,
        out_shape=slots,
        scratch_shapes=[
            pltpu.SMEM(tile_ranks.shape, tile_ranks.dtype),
            pltpu.VMEM(v_basis.shape, BF16),
            pltpu.VMEM(start_model.shape, F32),
            waves,
            padded_rows,
            pltpu.VMEM(slots.shape, BF16),
            pltpu.SemaphoreType.DMA((3,)),
            pltpu.SemaphoreType.DMA((2,)),
        ],
        compiler_params=params(60),
        name="first_projection",
    )(tile_ranks, v_basis, start_model)
    normal = normal_terms(phases, window_start, window_stop, records)
    in_hbm = lambda x: pltpu.with_memory_space_constraint(x, pltpu.HBM)
    fetch = [
        pltpu.VMEM(slots.shape, BF16),
        *[pltpu.VMEM(x.shape, F32) for x in normal],
        pltpu.VMEM((freqs, 2 * lanes, receivers), F32),
        pltpu.SemaphoreType.DMA((3,)),
    ]
    finish = [
        pltpu.VMEM(start_model.shape, F32),
        pltpu.SemaphoreType.DMA((len(chunks(points)),)),
    ]
    current = start_model
    for iteration in range(ITERS):
        cold = iteration == 0
        terms = [in_hbm(x) for x in normal] if cold else normal
        arrived = exchange(outgoing)
        outgoing = pl.pallas_call(
            functools.partial(misfit_kernel, pieces, cold),
            in_specs=[SMEM, HBM, VMEM, HBM, HBM] if cold else [SMEM] + [VMEM] * 4,
            out_specs=VMEM,
            out_shape=slots,
            scratch_shapes=[
                padded_rows,
                pltpu.VMEM((freqs, 2 * lanes, 2 * rank_total), BF16),
                pltpu.VMEM((freqs, 2, 2 * lanes, receivers), BF16),
            ]
            + (fetch if cold else []),
            compiler_params=params(8 + mebibytes(slots, *normal)),
            name="misfit",
        )(tile_ranks, arrived, u_basis, *terms)
        arrived = exchange(outgoing)
        last = iteration == ITERS - 1
        result = pl.pallas_call(
            functools.partial(update_kernel, pieces, last),
            in_specs=[SMEM] + [VMEM] * 3,
            out_specs=HBM if last else [VMEM, VMEM],
            out_shape=model if last else [model, slots],
            scratch_shapes=[padded_rows, left] + (finish if last else [waves]),
            compiler_params=params(12),
            name="last_update" if last else "update",
        )(tile_ranks, arrived, v_basis, current)
        if last:
            current = result
        else:
            current, outgoing = result
    return current


def solution(mesh):
    in_specs = (
        P(None, ("groups", "tile"), None),
        P(None, ("groups", "tile"), None),
        P(None, None, None, ("groups", "tile")),
        P(None, None, ("groups", "tile")),
        P("groups", None, None),
        P(None, ("groups", "tile")),
        P(None, ("groups", "tile")),
    )
    out_specs = P(None, ("groups", "tile"), None)
    return jax.shard_map(
        on_device, mesh=mesh, in_specs=in_specs, out_specs=out_specs, check_vma=False
    )
```

```python
import functools
import math

import jax
import jax.numpy as jnp
import numpy as np
from jax import lax
from jax.experimental import pallas as pl
from jax.experimental.pallas import tpu as pltpu
from jax.sharding import PartitionSpec as P

RMAX = 96
ITERS = 2
STEP = 0.5
START_MAX = 7
STOP_MIN = 16
STOP_MAX = 31
F32 = jnp.float32
BF16 = jnp.bfloat16

SMEM = pl.BlockSpec(memory_space=pltpu.SMEM)
VMEM = pl.BlockSpec(memory_space=pltpu.VMEM)
HBM = pl.BlockSpec(memory_space=pltpu.HBM)
MIB = 1024 * 1024


def mebibytes(*arrays):
    return sum(-(-x.size * x.dtype.itemsize // MIB) for x in arrays)


def params(mib):
    return pltpu.CompilerParams(vmem_limit_bytes=mib * MIB)


def phase_rows(freq_count, sample_count):
    moments = np.arange(sample_count, dtype=np.float64)
    bins = np.arange(freq_count, dtype=np.float64) + 1.0
    phases = 2.0 * math.pi / sample_count * bins[:, None] * moments[None, :]
    factor = math.sqrt(2.0 / sample_count)
    rows = np.stack([np.cos(phases), -np.sin(phases)], axis=1) * factor
    return rows.reshape(2 * freq_count, sample_count).astype(np.float32)


def pair_list(count):
    return [(a, b) for a in range(count) for b in range(a, count)]


def side_by_side(real, imag):
    return jnp.concatenate([real, imag], axis=1).astype(BF16)


def dot(left, right):
    return jnp.dot(left, right, preferred_element_type=F32)


def dot_last(left, right):
    return lax.dot_general(left, right, (((1,), (1,)), ((), ())), preferred_element_type=F32)


def above(upper, lower):
    return jnp.concatenate([upper, lower], axis=0).astype(BF16)


def running(ranks):
    starts = [0]
    for rank in ranks[:-1]:
        starts.append(starts[-1] + rank)
    return starts


def row_starts(ranks_ref, pieces):
    freqs, _, cols = ranks_ref.shape
    row = lax.axis_index("tile") // pieces
    return [running([ranks_ref[f, row, j] for j in range(cols)]) for f in range(freqs)]


def column_starts(ranks_ref):
    _, rows, cols = ranks_ref.shape
    device = lax.axis_index("tile")
    freq, col = device // cols, device % cols
    return running([ranks_ref[freq, i, col] for i in range(rows)])


def store_slots(starts, rows_ref, slots_ref, repeat, first_slot, done=None):
    for k, start in enumerate(starts):
        block = jnp.concatenate([rows_ref[c, pl.ds(start, RMAX), :] for c in range(2)], axis=1)
        block = block.astype(BF16)
        for p in range(repeat):
            slots_ref[first_slot + k * repeat + p] = block
            if done is not None:
                done(first_slot + k * repeat + p)


def piece_tree(blocks):
    while len(blocks) > 1:
        half = len(blocks) // 2
        blocks = [
            (blocks[q].astype(F32) + blocks[q + half].astype(F32)).astype(BF16)
            for q in range(half)
        ]
    return blocks[0]


def load_slots(starts, slots_ref, rows_ref, repeat, first_slot):
    lanes = rows_ref.shape[2]
    for k, start in enumerate(starts):
        block = piece_tree([slots_ref[first_slot + k * repeat + p] for p in range(repeat)])
        block = block.astype(F32)
        for c in range(2):
            rows_ref[c, pl.ds(start, RMAX), :] = block[:, c * lanes : (c + 1) * lanes]


def clear_tail(rows_ref, rank_total):
    tail = (2, rows_ref.shape[1] - rank_total, rows_ref.shape[2])
    rows_ref[:, rank_total:, :] = jnp.zeros(tail, F32)


def store_rows(rows_ref, rank_total, value):
    lanes = rows_ref.shape[2]
    for c in range(2):
        rows_ref[c, :rank_total, :] = value[:, c * lanes : (c + 1) * lanes]


def turned_stack(real, imag):
    return jnp.concatenate([side_by_side(*real), side_by_side(*imag)], axis=0).T


def chunks(width):
    size = math.gcd(width, 256)
    return [pl.ds(k, size) for k in range(0, width, size)]


def flat(block):
    return block.reshape(block.shape[0] * block.shape[1], block.shape[2])


def project(v_ref, waves_ref, rows_ref):
    value = dot(v_ref[0], waves_ref[0]) + dot(v_ref[1], waves_ref[1])
    store_rows(rows_ref, v_ref.shape[1], value)


def first_kernel(
    pieces,
    ranks_hbm,
    v_hbm,
    x_hbm,
    slots_hbm,
    ranks_ref,
    v_ref,
    x_ref,
    waves_ref,
    rows_ref,
    slots_ref,
    in_sems,
    out_sems,
):
    pairs = [(ranks_hbm, ranks_ref), (x_hbm, x_ref), (v_hbm, v_ref)]
    copies = [pltpu.make_async_copy(*pair, in_sems.at[n]) for n, pair in enumerate(pairs)]
    for copy in copies:
        copy.start()
    clear_tail(rows_ref, v_ref.shape[1])
    copies[1].wait()
    real, imag = x_ref[0], x_ref[1]
    waves_ref[0] = side_by_side(real, imag)
    waves_ref[1] = side_by_side(-imag, real)
    copies[2].wait()
    copies[0].wait()
    project(v_ref, waves_ref, rows_ref)
    sent = []

    def send(last_slot):
        group = slots_ref.shape[0] // out_sems.shape[0]
        if last_slot % group == group - 1:
            these = pl.ds(last_slot - group + 1, group)
            sem = out_sems.at[last_slot // group]
            sent.append(pltpu.make_async_copy(slots_ref.at[these], slots_hbm.at[these], sem))
            sent[-1].start()

    store_slots(column_starts(ranks_ref), rows_ref, slots_ref, pieces, 0, send)
    for copy in sent:
        copy.wait()


def misfit_kernel(
    pieces,
    cold,
    starts_ref,
    in_ref,
    u_ref,
    gram_ref,
    data_ref,
    *rest,
):
    freqs, rank_total, width = u_ref.shape[1:]
    cols = in_ref.shape[0] // freqs
    if cold:
        slots_hbm, gram_hbm, data_hbm = in_ref, gram_ref, data_ref
        out_ref, rows_ref, left_ref, field_ref, *fetch = rest
        ranks_hbm = starts_ref
        ranks_ref, in_ref, gram_ref, data_ref, pred_ref, sems = fetch
        pairs = [
            (ranks_hbm, ranks_ref),
            (slots_hbm, in_ref),
            (gram_hbm, gram_ref),
            (data_hbm, data_ref),
        ]
        copies = [pltpu.make_async_copy(*pair, sems.at[n]) for n, pair in enumerate(pairs)]
        for copy in copies:
            copy.start()
        copies[0].wait()
        copies[1].wait()
        starts = row_starts(ranks_ref, pieces)
    else:
        out_ref, rows_ref, left_ref, field_ref = rest
        starts = [[starts_ref[f * cols + j, 0] for j in range(cols)] for f in range(freqs)]
    lanes = in_ref.shape[2] // 2
    for f in range(freqs):
        load_slots(starts[f], in_ref, rows_ref, 1, f * cols)
        real, imag = rows_ref[0, :rank_total, :], rows_ref[1, :rank_total, :]
        left_ref[f] = turned_stack((real, imag), (-imag, real))
    parts = 2 * freqs
    where = {pair: k for k, pair in enumerate(pair_list(parts))}
    clear_tail(rows_ref, rank_total)
    if cold:
        for f in range(freqs):
            pred_ref[f] = dot(left_ref[f], flat(u_ref[:, f]))
        copies[2].wait()
        copies[3].wait()
    for some in chunks(width):
        preds = []
        for f in range(freqs):
            if cold:
                pred = pred_ref[f, :, some]
            else:
                pred = dot(left_ref[f], flat(u_ref[:, f, :, some]))
            preds += [pred[:lanes], pred[lanes:]]
        fields = []
        for a in range(parts):
            total = -data_ref[a, :, some]
            for b in range(parts):
                total = total + gram_ref[where[min(a, b), max(a, b)], :, some] * preds[b]
            fields.append(total)
        for f in range(freqs):
            real, imag = fields[2 * f], fields[2 * f + 1]
            field_ref[f, 0, :, some] = above(real, imag)
            field_ref[f, 1, :, some] = above(imag, -real)
    for f in range(freqs):
        value = dot_last(u_ref[0, f], field_ref[f, 0]) + dot_last(u_ref[1, f], field_ref[f, 1])
        store_rows(rows_ref, rank_total, value)
        store_slots(starts[f], rows_ref, out_ref, 1, f * cols)


def update_kernel(pieces, last, starts_ref, in_ref, v_ref, x_ref, *rest):
    if last:
        new_hbm, rows_ref, left_ref, new_ref, sems = rest
    else:
        new_ref, slots_ref, rows_ref, left_ref, waves_ref = rest
    rank_total, points = v_ref.shape[1:]
    lanes = in_ref.shape[2] // 2
    tiles = in_ref.shape[0]
    starts = [starts_ref[tiles + i, 0] for i in range(tiles // pieces)]
    load_slots(starts, in_ref, rows_ref, pieces, 0)
    real, imag = rows_ref[0, :rank_total, :], rows_ref[1, :rank_total, :]
    left_ref[...] = turned_stack((real, imag), (imag, -real))
    copies = []
    for k, some in enumerate(chunks(points)):
        gradient = dot(left_ref[...], flat(v_ref[:, :, some]))
        real = x_ref[0, some, :] - STEP * gradient[:lanes].T
        imag = x_ref[1, some, :] - STEP * gradient[lanes:].T
        new_ref[0, some, :] = real
        new_ref[1, some, :] = imag
        if last:
            copies.append(
                pltpu.make_async_copy(new_ref.at[:, some, :], new_hbm.at[:, some, :], sems.at[k])
            )
            copies[k].start()
        else:
            waves_ref[0, some, :] = side_by_side(real, imag)
            waves_ref[1, some, :] = side_by_side(-imag, real)
    if last:
        for copy in copies:
            copy.wait()
    else:
        clear_tail(rows_ref, rank_total)
        project(v_ref, waves_ref, rows_ref)
        store_slots(starts, rows_ref, slots_ref, pieces, 0)


def harmonic_sums(freq_count, sample_count):
    multiples = np.arange(2 * freq_count + 1, dtype=np.float64)[:, None]
    phases = 2.0 * math.pi / sample_count * multiples * np.arange(sample_count)[None, :]
    waves = np.stack([np.cos(phases), np.sin(phases)]) / sample_count
    sums = np.concatenate([np.zeros((2, waves.shape[1], 1)), np.cumsum(waves, axis=2)], axis=2)
    return sums.astype(np.float32)


def gram_parts(a, b):
    f, g = a // 2 + 1, b // 2 + 1
    apart, lean = abs(f - g), 1.0 if f > g else -1.0 if f < g else 0.0
    if a % 2 == 0 and b % 2 == 0:
        return [(0, apart, 1.0), (0, f + g, 1.0)]
    if a % 2 == 1 and b % 2 == 1:
        return [(0, apart, 1.0), (0, f + g, -1.0)]
    if a % 2 == 0:
        return [(1, apart, lean), (1, f + g, -1.0)]
    return [(1, apart, -lean), (1, f + g, -1.0)]


def normal_kernel(
    phases, pieces, ranks_ref, start_ref, stop_ref, records_ref, gram_ref, data_ref, starts_ref
):
    @pl.when(pl.program_id(0) == 0)
    def _():
        starts = sum(row_starts(ranks_ref, pieces), []) + column_starts(ranks_ref)
        for k, start in enumerate(starts):
            starts_ref[k, :] = jnp.full(starts_ref.shape[1:], start, jnp.int32)

    parts, samples = phases.shape
    half = samples // 2
    pairs = pair_list(parts)
    sums = harmonic_sums(parts // 2, samples)
    terms = [[term for term in gram_parts(a, b) if term[2] != 0.0] for a, b in pairs]
    needed = sorted({(kind, k) for some in terms for kind, k, _ in some if (kind, k) != (1, 0)})
    chunk = 16

    def pick(level, table, first, last):
        value = jnp.full(level.shape, float(table[first]), F32)
        for t in range(first + 1, last + 1):
            value = jnp.where(level >= t, float(table[t]), value)
        return value

    def add_up(step, carry):
        rows = pl.ds(pl.multiple_of(step * chunk, chunk), chunk)
        begin, end = start_ref[rows, :], stop_ref[rows, :]
        waves = {}
        for kind, k in needed:
            if (kind, k) == (0, 0):
                waves[kind, k] = (end - begin).astype(F32) * (1.0 / samples)
            else:
                table = sums[kind, k]
                waves[kind, k] = pick(end, table, STOP_MIN, STOP_MAX) - pick(
                    begin, table, 0, START_MAX
                )
        for n, some in enumerate(terms):
            total = None
            for kind, k, sign in some:
                if (kind, k) == (1, 0):
                    continue
                if total is None:
                    total = waves[kind, k] if sign > 0 else -waves[kind, k]
                else:
                    total = total + waves[kind, k] if sign > 0 else total - waves[kind, k]
            gram_ref[n, rows, :] = total

        def seen(t):
            value = records_ref[t, rows, :].astype(F32)
            if t < START_MAX:
                value = jnp.where(begin <= t, value, 0.0)
            if t >= STOP_MIN:
                value = jnp.where(end > t, value, 0.0)
            return value

        for odd in (0, 1):
            some = [a for a in range(parts) if (a // 2 + 1) % 2 == odd]
            datas = [jnp.zeros(begin.shape, F32) for _ in some]
            for t in range(half if some else 0):
                late, early = t + half, seen(t)
                if late < STOP_MAX:
                    early = early - seen(late) if odd else early + seen(late)
                for k, a in enumerate(some):
                    datas[k] = datas[k] + float(phases[a, t]) * early
            for k, a in enumerate(some):
                data_ref[a, rows, :] = datas[k]
        return carry

    lax.fori_loop(0, start_ref.shape[0] // chunk, add_up, 0)


def normal_terms(phases, pieces, tile_ranks, window_start, window_stop, records):
    samples, lanes, width = records.shape
    parts = phases.shape[0]
    pair_count = len(pair_list(parts))
    block = 128
    freqs, rows, cols = tile_ranks.shape
    starts = (freqs * cols + rows, block)
    return pl.pallas_call(
        functools.partial(normal_kernel, phases, pieces),
        grid=(width // block,),
        in_specs=[
            SMEM,
            pl.BlockSpec((lanes, block), lambda n: (0, n)),
            pl.BlockSpec((lanes, block), lambda n: (0, n)),
            pl.BlockSpec((samples, lanes, block), lambda n: (0, 0, n)),
        ],
        out_specs=[
            pl.BlockSpec((pair_count, lanes, block), lambda n: (0, 0, n)),
            pl.BlockSpec((parts, lanes, block), lambda n: (0, 0, n)),
            pl.BlockSpec(starts, lambda n: (0, 0)),
        ],
        out_shape=[
            jax.ShapeDtypeStruct((pair_count, lanes, width), F32),
            jax.ShapeDtypeStruct((parts, lanes, width), F32),
            jax.ShapeDtypeStruct(starts, jnp.int32),
        ],
        cost_estimate=pl.CostEstimate(
            flops=16 * records.size, bytes_accessed=3 * records.size, transcendentals=0
        ),
        compiler_params=params(60),
        name="normal_terms",
    )(tile_ranks, window_start, window_stop, records)


def on_device(start_model, v_basis, u_basis, records, tile_ranks, window_start, window_stop):
    tiles = lax.axis_size("tile")
    freqs, rows, cols = tile_ranks.shape
    pieces = tiles // rows
    rank_total = v_basis.shape[1]
    points, lanes = start_model.shape[1:]
    receivers = u_basis.shape[3]
    phases = phase_rows(freqs, records.shape[0])

    slots = jax.ShapeDtypeStruct((tiles, RMAX, 2 * lanes), BF16)
    model = jax.ShapeDtypeStruct(start_model.shape, F32)
    padded_rows = pltpu.VMEM((2, rank_total + RMAX, lanes), F32)
    waves = pltpu.VMEM((2, points, 2 * lanes), BF16)
    left = pltpu.VMEM((2 * lanes, 2 * rank_total), BF16)
    exchange = lambda x: lax.all_to_all(x, "tile", split_axis=0, concat_axis=0, tiled=True)

    outgoing = pl.pallas_call(
        functools.partial(first_kernel, pieces),
        in_specs=[HBM, HBM, HBM],
        out_specs=HBM,
        out_shape=slots,
        scratch_shapes=[
            pltpu.SMEM(tile_ranks.shape, tile_ranks.dtype),
            pltpu.VMEM(v_basis.shape, BF16),
            pltpu.VMEM(start_model.shape, F32),
            waves,
            padded_rows,
            pltpu.VMEM(slots.shape, BF16),
            pltpu.SemaphoreType.DMA((3,)),
            pltpu.SemaphoreType.DMA((2,)),
        ],
        compiler_params=params(60),
        name="first_projection",
    )(tile_ranks, v_basis, start_model)
    *normal, starts = normal_terms(
        phases, pieces, tile_ranks, window_start, window_stop, records
    )
    in_hbm = lambda x: pltpu.with_memory_space_constraint(x, pltpu.HBM)
    fetch = [
        pltpu.SMEM(tile_ranks.shape, tile_ranks.dtype),
        pltpu.VMEM(slots.shape, BF16),
        *[pltpu.VMEM(x.shape, F32) for x in normal],
        pltpu.VMEM((freqs, 2 * lanes, receivers), F32),
        pltpu.SemaphoreType.DMA((4,)),
    ]
    finish = [
        pltpu.VMEM(start_model.shape, F32),
        pltpu.SemaphoreType.DMA((len(chunks(points)),)),
    ]
    current = start_model
    for iteration in range(ITERS):
        cold = iteration == 0
        terms = [in_hbm(x) for x in normal] if cold else normal
        arrived = exchange(outgoing)
        outgoing = pl.pallas_call(
            functools.partial(misfit_kernel, pieces, cold),
            in_specs=[HBM, HBM, VMEM, HBM, HBM] if cold else [VMEM] * 5,
            out_specs=VMEM,
            out_shape=slots,
            scratch_shapes=[
                padded_rows,
                pltpu.VMEM((freqs, 2 * lanes, 2 * rank_total), BF16),
                pltpu.VMEM((freqs, 2, 2 * lanes, receivers), BF16),
            ]
            + (fetch if cold else []),
            compiler_params=params(8 + mebibytes(slots, *normal)),
            name="misfit",
        )(tile_ranks if cold else starts, arrived, u_basis, *terms)
        arrived = exchange(outgoing)
        last = iteration == ITERS - 1
        result = pl.pallas_call(
            functools.partial(update_kernel, pieces, last),
            in_specs=[VMEM] * 4,
            out_specs=HBM if last else [VMEM, VMEM],
            out_shape=model if last else [model, slots],
            scratch_shapes=[padded_rows, left] + (finish if last else [waves]),
            compiler_params=params(12),
            name="last_update" if last else "update",
        )(starts, arrived, v_basis, current)
        if last:
            current = result
        else:
            current, outgoing = result
    return current


def solution(mesh):
    in_specs = (
        P(None, ("groups", "tile"), None),
        P(None, ("groups", "tile"), None),
        P(None, None, None, ("groups", "tile")),
        P(None, None, ("groups", "tile")),
        P("groups", None, None),
        P(None, ("groups", "tile")),
        P(None, ("groups", "tile")),
    )
    out_specs = P(None, ("groups", "tile"), None)
    return jax.shard_map(
        on_device, mesh=mesh, in_specs=in_specs, out_specs=out_specs, check_vma=False
    )
```

```python
import functools
import math

import jax
import jax.numpy as jnp
import numpy as np
from jax import lax
from jax.experimental import pallas as pl
from jax.experimental.pallas import tpu as pltpu
from jax.sharding import PartitionSpec as P

RMAX = 96
ITERS = 2
STEP = 0.5
START_MAX = 7
STOP_MIN = 16
STOP_MAX = 31
F32 = jnp.float32
BF16 = jnp.bfloat16

SMEM = pl.BlockSpec(memory_space=pltpu.SMEM)
VMEM = pl.BlockSpec(memory_space=pltpu.VMEM)
HBM = pl.BlockSpec(memory_space=pltpu.HBM)
MIB = 1024 * 1024


def mebibytes(*arrays):
    return sum(-(-x.size * x.dtype.itemsize // MIB) for x in arrays)


def params(mib):
    return pltpu.CompilerParams(vmem_limit_bytes=mib * MIB)


def phase_rows(freq_count, sample_count):
    moments = np.arange(sample_count, dtype=np.float64)
    bins = np.arange(freq_count, dtype=np.float64) + 1.0
    phases = 2.0 * math.pi / sample_count * bins[:, None] * moments[None, :]
    factor = math.sqrt(2.0 / sample_count)
    rows = np.stack([np.cos(phases), -np.sin(phases)], axis=1) * factor
    return rows.reshape(2 * freq_count, sample_count).astype(np.float32)


def pair_list(count):
    return [(a, b) for a in range(count) for b in range(a, count)]


def side_by_side(real, imag):
    return jnp.concatenate([real, imag], axis=1).astype(BF16)


def dot(left, right):
    return jnp.dot(left, right, preferred_element_type=F32)


def dot_last(left, right):
    return lax.dot_general(left, right, (((1,), (1,)), ((), ())), preferred_element_type=F32)


def above(upper, lower):
    return jnp.concatenate([upper, lower], axis=0).astype(BF16)


def running(ranks):
    starts = [0]
    for rank in ranks[:-1]:
        starts.append(starts[-1] + rank)
    return starts


def row_starts(ranks_ref, pieces):
    freqs, _, cols = ranks_ref.shape
    row = lax.axis_index("tile") // pieces
    return [running([ranks_ref[f, row, j] for j in range(cols)]) for f in range(freqs)]


def column_starts(ranks_ref):
    _, rows, cols = ranks_ref.shape
    device = lax.axis_index("tile")
    freq, col = device // cols, device % cols
    return running([ranks_ref[freq, i, col] for i in range(rows)])


def store_slots(starts, rows_ref, slots_ref, repeat, first_slot, done=None):
    for k, start in enumerate(starts):
        block = jnp.concatenate([rows_ref[c, pl.ds(start, RMAX), :] for c in range(2)], axis=1)
        block = block.astype(BF16)
        for p in range(repeat):
            slots_ref[first_slot + k * repeat + p] = block
            if done is not None:
                done(first_slot + k * repeat + p)


def piece_tree(blocks):
    while len(blocks) > 1:
        half = len(blocks) // 2
        blocks = [
            (blocks[q].astype(F32) + blocks[q + half].astype(F32)).astype(BF16)
            for q in range(half)
        ]
    return blocks[0]


def load_slots(starts, slots_ref, rows_ref, repeat, first_slot):
    lanes = rows_ref.shape[2]
    for k, start in enumerate(starts):
        block = piece_tree([slots_ref[first_slot + k * repeat + p] for p in range(repeat)])
        block = block.astype(F32)
        for c in range(2):
            rows_ref[c, pl.ds(start, RMAX), :] = block[:, c * lanes : (c + 1) * lanes]


def clear_tail(rows_ref, rank_total):
    tail = (2, rows_ref.shape[1] - rank_total, rows_ref.shape[2])
    rows_ref[:, rank_total:, :] = jnp.zeros(tail, F32)


def store_rows(rows_ref, rank_total, value):
    lanes = rows_ref.shape[2]
    for c in range(2):
        rows_ref[c, :rank_total, :] = value[:, c * lanes : (c + 1) * lanes]


def turned_stack(real, imag):
    return jnp.concatenate([side_by_side(*real), side_by_side(*imag)], axis=0).T


def chunks(width):
    size = math.gcd(width, 256)
    return [pl.ds(k, size) for k in range(0, width, size)]


def flat(block):
    return block.reshape(block.shape[0] * block.shape[1], block.shape[2])


def project(v_ref, waves_ref, rows_ref):
    value = dot(v_ref[0], waves_ref[0]) + dot(v_ref[1], waves_ref[1])
    store_rows(rows_ref, v_ref.shape[1], value)


def first_kernel(
    pieces,
    ranks_hbm,
    v_hbm,
    x_hbm,
    slots_hbm,
    ranks_ref,
    v_ref,
    x_ref,
    waves_ref,
    rows_ref,
    slots_ref,
    in_sems,
    out_sems,
):
    pairs = [(ranks_hbm, ranks_ref), (x_hbm, x_ref), (v_hbm, v_ref)]
    copies = [pltpu.make_async_copy(*pair, in_sems.at[n]) for n, pair in enumerate(pairs)]
    for copy in copies:
        copy.start()
    clear_tail(rows_ref, v_ref.shape[1])
    copies[1].wait()
    real, imag = x_ref[0], x_ref[1]
    waves_ref[0] = side_by_side(real, imag)
    waves_ref[1] = side_by_side(-imag, real)
    copies[2].wait()
    copies[0].wait()
    project(v_ref, waves_ref, rows_ref)
    sent = []

    def send(last_slot):
        group = slots_ref.shape[0] // out_sems.shape[0]
        if last_slot % group == group - 1:
            these = pl.ds(last_slot - group + 1, group)
            sem = out_sems.at[last_slot // group]
            sent.append(pltpu.make_async_copy(slots_ref.at[these], slots_hbm.at[these], sem))
            sent[-1].start()

    store_slots(column_starts(ranks_ref), rows_ref, slots_ref, pieces, 0, send)
    for copy in sent:
        copy.wait()


def misfit_kernel(
    pieces,
    cold,
    starts_ref,
    in_ref,
    u_ref,
    gram_ref,
    data_ref,
    *rest,
):
    freqs, rank_total, width = u_ref.shape[1:]
    cols = in_ref.shape[0] // freqs
    if cold:
        slots_hbm, gram_hbm, data_hbm = in_ref, gram_ref, data_ref
        v_hbm, x_hbm, out_ref, v_ref, x_ref, rows_ref, left_ref, field_ref, *fetch = rest
        ranks_hbm = starts_ref
        ranks_ref, in_ref, gram_ref, data_ref, pred_ref, sems = fetch
        pairs = [
            (ranks_hbm, ranks_ref),
            (slots_hbm, in_ref),
            (gram_hbm, gram_ref),
            (data_hbm, data_ref),
            (v_hbm, v_ref),
            (x_hbm, x_ref),
        ]
        copies = [pltpu.make_async_copy(*pair, sems.at[n]) for n, pair in enumerate(pairs)]
        for copy in copies:
            copy.start()
        copies[0].wait()
        copies[1].wait()
        starts = row_starts(ranks_ref, pieces)
    else:
        out_ref, rows_ref, left_ref, field_ref = rest
        starts = [[starts_ref[f * cols + j, 0] for j in range(cols)] for f in range(freqs)]
    lanes = in_ref.shape[2] // 2
    for f in range(freqs):
        load_slots(starts[f], in_ref, rows_ref, 1, f * cols)
        real, imag = rows_ref[0, :rank_total, :], rows_ref[1, :rank_total, :]
        left_ref[f] = turned_stack((real, imag), (-imag, real))
    parts = 2 * freqs
    where = {pair: k for k, pair in enumerate(pair_list(parts))}
    clear_tail(rows_ref, rank_total)
    if cold:
        for f in range(freqs):
            pred_ref[f] = dot(left_ref[f], flat(u_ref[:, f]))
        copies[2].wait()
        copies[3].wait()
    for some in chunks(width):
        preds = []
        for f in range(freqs):
            if cold:
                pred = pred_ref[f, :, some]
            else:
                pred = dot(left_ref[f], flat(u_ref[:, f, :, some]))
            preds += [pred[:lanes], pred[lanes:]]
        fields = []
        for a in range(parts):
            total = -data_ref[a, :, some]
            for b in range(parts):
                total = total + gram_ref[where[min(a, b), max(a, b)], :, some] * preds[b]
            fields.append(total)
        for f in range(freqs):
            real, imag = fields[2 * f], fields[2 * f + 1]
            field_ref[f, 0, :, some] = above(real, imag)
            field_ref[f, 1, :, some] = above(imag, -real)
    for f in range(freqs):
        value = dot_last(u_ref[0, f], field_ref[f, 0]) + dot_last(u_ref[1, f], field_ref[f, 1])
        store_rows(rows_ref, rank_total, value)
        store_slots(starts[f], rows_ref, out_ref, 1, f * cols)
    if cold:
        copies[4].wait()
        copies[5].wait()


def update_kernel(pieces, last, starts_ref, in_ref, v_ref, x_ref, *rest):
    if last:
        new_hbm, rows_ref, left_ref, new_ref, sems = rest
    else:
        new_ref, slots_ref, rows_ref, left_ref, waves_ref = rest
    rank_total, points = v_ref.shape[1:]
    lanes = in_ref.shape[2] // 2
    tiles = in_ref.shape[0]
    starts = [starts_ref[tiles + i, 0] for i in range(tiles // pieces)]
    load_slots(starts, in_ref, rows_ref, pieces, 0)
    real, imag = rows_ref[0, :rank_total, :], rows_ref[1, :rank_total, :]
    left_ref[...] = turned_stack((real, imag), (imag, -real))
    copies = []
    for k, some in enumerate(chunks(points)):
        gradient = dot(left_ref[...], flat(v_ref[:, :, some]))
        real = x_ref[0, some, :] - STEP * gradient[:lanes].T
        imag = x_ref[1, some, :] - STEP * gradient[lanes:].T
        new_ref[0, some, :] = real
        new_ref[1, some, :] = imag
        if last:
            copies.append(
                pltpu.make_async_copy(new_ref.at[:, some, :], new_hbm.at[:, some, :], sems.at[k])
            )
            copies[k].start()
        else:
            waves_ref[0, some, :] = side_by_side(real, imag)
            waves_ref[1, some, :] = side_by_side(-imag, real)
    if last:
        for copy in copies:
            copy.wait()
    else:
        clear_tail(rows_ref, rank_total)
        project(v_ref, waves_ref, rows_ref)
        store_slots(starts, rows_ref, slots_ref, pieces, 0)


def harmonic_sums(freq_count, sample_count):
    multiples = np.arange(2 * freq_count + 1, dtype=np.float64)[:, None]
    phases = 2.0 * math.pi / sample_count * multiples * np.arange(sample_count)[None, :]
    waves = np.stack([np.cos(phases), np.sin(phases)]) / sample_count
    sums = np.concatenate([np.zeros((2, waves.shape[1], 1)), np.cumsum(waves, axis=2)], axis=2)
    return sums.astype(np.float32)


def gram_parts(a, b):
    f, g = a // 2 + 1, b // 2 + 1
    apart, lean = abs(f - g), 1.0 if f > g else -1.0 if f < g else 0.0
    if a % 2 == 0 and b % 2 == 0:
        return [(0, apart, 1.0), (0, f + g, 1.0)]
    if a % 2 == 1 and b % 2 == 1:
        return [(0, apart, 1.0), (0, f + g, -1.0)]
    if a % 2 == 0:
        return [(1, apart, lean), (1, f + g, -1.0)]
    return [(1, apart, -lean), (1, f + g, -1.0)]


def normal_kernel(
    phases, pieces, ranks_ref, start_ref, stop_ref, records_ref, gram_ref, data_ref, starts_ref
):
    @pl.when(pl.program_id(0) == 0)
    def _():
        starts = sum(row_starts(ranks_ref, pieces), []) + column_starts(ranks_ref)
        for k, start in enumerate(starts):
            starts_ref[k, :] = jnp.full(starts_ref.shape[1:], start, jnp.int32)

    parts, samples = phases.shape
    half = samples // 2
    pairs = pair_list(parts)
    sums = harmonic_sums(parts // 2, samples)
    terms = [[term for term in gram_parts(a, b) if term[2] != 0.0] for a, b in pairs]
    needed = sorted({(kind, k) for some in terms for kind, k, _ in some if (kind, k) != (1, 0)})
    chunk = 16

    def pick(level, table, first, last):
        value = jnp.full(level.shape, float(table[first]), F32)
        for t in range(first + 1, last + 1):
            value = jnp.where(level >= t, float(table[t]), value)
        return value

    def add_up(step, carry):
        rows = pl.ds(pl.multiple_of(step * chunk, chunk), chunk)
        begin, end = start_ref[rows, :], stop_ref[rows, :]
        waves = {}
        for kind, k in needed:
            if (kind, k) == (0, 0):
                waves[kind, k] = (end - begin).astype(F32) * (1.0 / samples)
            else:
                table = sums[kind, k]
                waves[kind, k] = pick(end, table, STOP_MIN, STOP_MAX) - pick(
                    begin, table, 0, START_MAX
                )
        for n, some in enumerate(terms):
            total = None
            for kind, k, sign in some:
                if (kind, k) == (1, 0):
                    continue
                if total is None:
                    total = waves[kind, k] if sign > 0 else -waves[kind, k]
                else:
                    total = total + waves[kind, k] if sign > 0 else total - waves[kind, k]
            gram_ref[n, rows, :] = total

        def seen(t):
            value = records_ref[t, rows, :].astype(F32)
            if t < START_MAX:
                value = jnp.where(begin <= t, value, 0.0)
            if t >= STOP_MIN:
                value = jnp.where(end > t, value, 0.0)
            return value

        for odd in (0, 1):
            some = [a for a in range(parts) if (a // 2 + 1) % 2 == odd]
            datas = [jnp.zeros(begin.shape, F32) for _ in some]
            for t in range(half if some else 0):
                late, early = t + half, seen(t)
                if late < STOP_MAX:
                    early = early - seen(late) if odd else early + seen(late)
                for k, a in enumerate(some):
                    datas[k] = datas[k] + float(phases[a, t]) * early
            for k, a in enumerate(some):
                data_ref[a, rows, :] = datas[k]
        return carry

    lax.fori_loop(0, start_ref.shape[0] // chunk, add_up, 0)


def normal_terms(phases, pieces, tile_ranks, window_start, window_stop, records):
    samples, lanes, width = records.shape
    parts = phases.shape[0]
    pair_count = len(pair_list(parts))
    block = 128
    freqs, rows, cols = tile_ranks.shape
    starts = (freqs * cols + rows, block)
    return pl.pallas_call(
        functools.partial(normal_kernel, phases, pieces),
        grid=(width // block,),
        in_specs=[
            SMEM,
            pl.BlockSpec((lanes, block), lambda n: (0, n)),
            pl.BlockSpec((lanes, block), lambda n: (0, n)),
            pl.BlockSpec((samples, lanes, block), lambda n: (0, 0, n)),
        ],
        out_specs=[
            pl.BlockSpec((pair_count, lanes, block), lambda n: (0, 0, n)),
            pl.BlockSpec((parts, lanes, block), lambda n: (0, 0, n)),
            pl.BlockSpec(starts, lambda n: (0, 0)),
        ],
        out_shape=[
            jax.ShapeDtypeStruct((pair_count, lanes, width), F32),
            jax.ShapeDtypeStruct((parts, lanes, width), F32),
            jax.ShapeDtypeStruct(starts, jnp.int32),
        ],
        cost_estimate=pl.CostEstimate(
            flops=16 * records.size, bytes_accessed=3 * records.size, transcendentals=0
        ),
        compiler_params=params(60),
        name="normal_terms",
    )(tile_ranks, window_start, window_stop, records)


def on_device(start_model, v_basis, u_basis, records, tile_ranks, window_start, window_stop):
    tiles = lax.axis_size("tile")
    freqs, rows, cols = tile_ranks.shape
    pieces = tiles // rows
    rank_total = v_basis.shape[1]
    points, lanes = start_model.shape[1:]
    receivers = u_basis.shape[3]
    phases = phase_rows(freqs, records.shape[0])

    slots = jax.ShapeDtypeStruct((tiles, RMAX, 2 * lanes), BF16)
    model = jax.ShapeDtypeStruct(start_model.shape, F32)
    v_like = jax.ShapeDtypeStruct(v_basis.shape, BF16)
    padded_rows = pltpu.VMEM((2, rank_total + RMAX, lanes), F32)
    waves = pltpu.VMEM((2, points, 2 * lanes), BF16)
    left = pltpu.VMEM((2 * lanes, 2 * rank_total), BF16)
    exchange = lambda x: lax.all_to_all(x, "tile", split_axis=0, concat_axis=0, tiled=True)

    outgoing = pl.pallas_call(
        functools.partial(first_kernel, pieces),
        in_specs=[HBM, HBM, HBM],
        out_specs=HBM,
        out_shape=slots,
        scratch_shapes=[
            pltpu.SMEM(tile_ranks.shape, tile_ranks.dtype),
            pltpu.VMEM(v_basis.shape, BF16),
            pltpu.VMEM(start_model.shape, F32),
            waves,
            padded_rows,
            pltpu.VMEM(slots.shape, BF16),
            pltpu.SemaphoreType.DMA((3,)),
            pltpu.SemaphoreType.DMA((2,)),
        ],
        compiler_params=params(60),
        name="first_projection",
    )(tile_ranks, v_basis, start_model)
    *normal, starts = normal_terms(
        phases, pieces, tile_ranks, window_start, window_stop, records
    )
    in_hbm = lambda x: pltpu.with_memory_space_constraint(x, pltpu.HBM)
    fetch = [
        pltpu.SMEM(tile_ranks.shape, tile_ranks.dtype),
        pltpu.VMEM(slots.shape, BF16),
        *[pltpu.VMEM(x.shape, F32) for x in normal],
        pltpu.VMEM((freqs, 2 * lanes, receivers), F32),
        pltpu.SemaphoreType.DMA((6,)),
    ]
    finish = [
        pltpu.VMEM(start_model.shape, F32),
        pltpu.SemaphoreType.DMA((len(chunks(points)),)),
    ]
    current = start_model
    for iteration in range(ITERS):
        cold = iteration == 0
        terms = [in_hbm(x) for x in normal] if cold else normal
        early = [in_hbm(v_basis), in_hbm(current)] if cold else []
        arrived = exchange(outgoing)
        result = pl.pallas_call(
            functools.partial(misfit_kernel, pieces, cold),
            in_specs=[HBM, HBM, VMEM, HBM, HBM, HBM, HBM] if cold else [VMEM] * 5,
            out_specs=[VMEM] * 3 if cold else VMEM,
            out_shape=[slots, v_like, model] if cold else slots,
            scratch_shapes=[
                padded_rows,
                pltpu.VMEM((freqs, 2 * lanes, 2 * rank_total), BF16),
                pltpu.VMEM((freqs, 2, 2 * lanes, receivers), BF16),
            ]
            + (fetch if cold else []),
            compiler_params=params(8 + mebibytes(slots, v_basis, model, *normal)),
            name="misfit",
        )(tile_ranks if cold else starts, arrived, u_basis, *terms, *early)
        if cold:
            outgoing, v_basis, current = result
        else:
            outgoing = result
        arrived = exchange(outgoing)
        last = iteration == ITERS - 1
        result = pl.pallas_call(
            functools.partial(update_kernel, pieces, last),
            in_specs=[VMEM] * 4,
            out_specs=HBM if last else [VMEM, VMEM],
            out_shape=model if last else [model, slots],
            scratch_shapes=[padded_rows, left] + (finish if last else [waves]),
            compiler_params=params(12),
            name="last_update" if last else "update",
        )(starts, arrived, v_basis, current)
        if last:
            current = result
        else:
            current, outgoing = result
    return current


def solution(mesh):
    in_specs = (
        P(None, ("groups", "tile"), None),
        P(None, ("groups", "tile"), None),
        P(None, None, None, ("groups", "tile")),
        P(None, None, ("groups", "tile")),
        P("groups", None, None),
        P(None, ("groups", "tile")),
        P(None, ("groups", "tile")),
    )
    out_specs = P(None, ("groups", "tile"), None)
    return jax.shard_map(
        on_device, mesh=mesh, in_specs=in_specs, out_specs=out_specs, check_vma=False
    )
```

```python
import functools
import math

import jax
import jax.numpy as jnp
import numpy as np
from jax import lax
from jax.experimental import pallas as pl
from jax.experimental.pallas import tpu as pltpu
from jax.sharding import PartitionSpec as P

RMAX = 96
ITERS = 2
STEP = 0.5
START_MAX = 7
STOP_MIN = 16
STOP_MAX = 31
F32 = jnp.float32
BF16 = jnp.bfloat16

SMEM = pl.BlockSpec(memory_space=pltpu.SMEM)
VMEM = pl.BlockSpec(memory_space=pltpu.VMEM)
HBM = pl.BlockSpec(memory_space=pltpu.HBM)
MIB = 1024 * 1024


def mebibytes(*arrays):
    return sum(-(-x.size * x.dtype.itemsize // MIB) for x in arrays)


def params(mib):
    return pltpu.CompilerParams(vmem_limit_bytes=mib * MIB)


def phase_rows(freq_count, sample_count):
    moments = np.arange(sample_count, dtype=np.float64)
    bins = np.arange(freq_count, dtype=np.float64) + 1.0
    phases = 2.0 * math.pi / sample_count * bins[:, None] * moments[None, :]
    factor = math.sqrt(2.0 / sample_count)
    rows = np.stack([np.cos(phases), -np.sin(phases)], axis=1) * factor
    return rows.reshape(2 * freq_count, sample_count).astype(np.float32)


def pair_list(count):
    return [(a, b) for a in range(count) for b in range(a, count)]


def side_by_side(real, imag):
    return jnp.concatenate([real, imag], axis=1).astype(BF16)


def dot(left, right):
    return jnp.dot(left, right, preferred_element_type=F32)


def dot_last(left, right):
    return lax.dot_general(left, right, (((1,), (1,)), ((), ())), preferred_element_type=F32)


def above(upper, lower):
    return jnp.concatenate([upper, lower], axis=0).astype(BF16)


def running(ranks):
    starts = [0]
    for rank in ranks[:-1]:
        starts.append(starts[-1] + rank)
    return starts


def row_starts(ranks_ref, pieces):
    freqs, _, cols = ranks_ref.shape
    row = lax.axis_index("tile") // pieces
    return [running([ranks_ref[f, row, j] for j in range(cols)]) for f in range(freqs)]


def column_starts(ranks_ref):
    _, rows, cols = ranks_ref.shape
    device = lax.axis_index("tile")
    freq, col = device // cols, device % cols
    return running([ranks_ref[freq, i, col] for i in range(rows)])


def store_slots(starts, rows_ref, slots_ref, repeat, first_slot, done=None):
    for k, start in enumerate(starts):
        block = jnp.concatenate([rows_ref[c, pl.ds(start, RMAX), :] for c in range(2)], axis=1)
        block = block.astype(BF16)
        for p in range(repeat):
            slots_ref[first_slot + k * repeat + p] = block
            if done is not None:
                done(first_slot + k * repeat + p)


def piece_tree(blocks):
    while len(blocks) > 1:
        half = len(blocks) // 2
        blocks = [
            (blocks[q].astype(F32) + blocks[q + half].astype(F32)).astype(BF16)
            for q in range(half)
        ]
    return blocks[0]


def load_slots(starts, slots_ref, rows_ref, repeat, first_slot):
    lanes = rows_ref.shape[2]
    for k, start in enumerate(starts):
        block = piece_tree([slots_ref[first_slot + k * repeat + p] for p in range(repeat)])
        block = block.astype(F32)
        for c in range(2):
            rows_ref[c, pl.ds(start, RMAX), :] = block[:, c * lanes : (c + 1) * lanes]


def clear_tail(rows_ref, rank_total):
    tail = (2, rows_ref.shape[1] - rank_total, rows_ref.shape[2])
    rows_ref[:, rank_total:, :] = jnp.zeros(tail, F32)


def store_rows(rows_ref, rank_total, value):
    lanes = rows_ref.shape[2]
    for c in range(2):
        rows_ref[c, :rank_total, :] = value[:, c * lanes : (c + 1) * lanes]


def turned_stack(real, imag):
    return jnp.concatenate([side_by_side(*real), side_by_side(*imag)], axis=0).T


def chunks(width):
    size = math.gcd(width, 256)
    return [pl.ds(k, size) for k in range(0, width, size)]


def flat(block):
    return block.reshape(block.shape[0] * block.shape[1], block.shape[2])


def project(v_ref, waves_ref, rows_ref):
    value = dot(v_ref[0], waves_ref[0]) + dot(v_ref[1], waves_ref[1])
    store_rows(rows_ref, v_ref.shape[1], value)


def first_kernel(
    pieces,
    ranks_hbm,
    v_hbm,
    x_hbm,
    slots_hbm,
    ranks_ref,
    v_ref,
    x_ref,
    waves_ref,
    rows_ref,
    slots_ref,
    in_sems,
    out_sems,
):
    pairs = [(ranks_hbm, ranks_ref), (x_hbm, x_ref), (v_hbm, v_ref)]
    copies = [pltpu.make_async_copy(*pair, in_sems.at[n]) for n, pair in enumerate(pairs)]
    for copy in copies:
        copy.start()
    clear_tail(rows_ref, v_ref.shape[1])
    copies[1].wait()
    real, imag = x_ref[0], x_ref[1]
    waves_ref[0] = side_by_side(real, imag)
    waves_ref[1] = side_by_side(-imag, real)
    copies[2].wait()
    copies[0].wait()
    project(v_ref, waves_ref, rows_ref)
    sent = []

    def send(last_slot):
        group = slots_ref.shape[0] // out_sems.shape[0]
        if last_slot % group == group - 1:
            these = pl.ds(last_slot - group + 1, group)
            sem = out_sems.at[last_slot // group]
            sent.append(pltpu.make_async_copy(slots_ref.at[these], slots_hbm.at[these], sem))
            sent[-1].start()

    store_slots(column_starts(ranks_ref), rows_ref, slots_ref, pieces, 0, send)
    for copy in sent:
        copy.wait()


def misfit_kernel(
    pieces,
    cold,
    starts_ref,
    in_ref,
    u_ref,
    gram_ref,
    data_ref,
    *rest,
):
    freqs, rank_total, width = u_ref.shape[1:]
    cols = in_ref.shape[0] // freqs
    if cold:
        slots_hbm, gram_hbm, data_hbm = in_ref, gram_ref, data_ref
        v_hbm, x_hbm, out_ref, v_ref, x_ref, rows_ref, left_ref, field_ref, *fetch = rest
        ranks_hbm = starts_ref
        ranks_ref, in_ref, gram_ref, data_ref, pred_ref, sems = fetch
        pairs = [
            (ranks_hbm, ranks_ref),
            (slots_hbm, in_ref),
            (gram_hbm, gram_ref),
            (data_hbm, data_ref),
            (v_hbm, v_ref),
            (x_hbm, x_ref),
        ]
        copies = [pltpu.make_async_copy(*pair, sems.at[n]) for n, pair in enumerate(pairs)]
        for copy in copies[:4]:
            copy.start()
        copies[0].wait()
        copies[1].wait()
        for copy in copies[4:]:
            copy.start()
        starts = row_starts(ranks_ref, pieces)
    else:
        out_ref, rows_ref, left_ref, field_ref = rest
        starts = [[starts_ref[f * cols + j, 0] for j in range(cols)] for f in range(freqs)]
    lanes = in_ref.shape[2] // 2
    for f in range(freqs):
        load_slots(starts[f], in_ref, rows_ref, 1, f * cols)
        real, imag = rows_ref[0, :rank_total, :], rows_ref[1, :rank_total, :]
        left_ref[f] = turned_stack((real, imag), (-imag, real))
    parts = 2 * freqs
    where = {pair: k for k, pair in enumerate(pair_list(parts))}
    clear_tail(rows_ref, rank_total)
    if cold:
        for f in range(freqs):
            pred_ref[f] = dot(left_ref[f], flat(u_ref[:, f]))
        copies[2].wait()
        copies[3].wait()
    for some in chunks(width):
        preds = []
        for f in range(freqs):
            if cold:
                pred = pred_ref[f, :, some]
            else:
                pred = dot(left_ref[f], flat(u_ref[:, f, :, some]))
            preds += [pred[:lanes], pred[lanes:]]
        fields = []
        for a in range(parts):
            total = -data_ref[a, :, some]
            for b in range(parts):
                total = total + gram_ref[where[min(a, b), max(a, b)], :, some] * preds[b]
            fields.append(total)
        for f in range(freqs):
            real, imag = fields[2 * f], fields[2 * f + 1]
            field_ref[f, 0, :, some] = above(real, imag)
            field_ref[f, 1, :, some] = above(imag, -real)
    for f in range(freqs):
        value = dot_last(u_ref[0, f], field_ref[f, 0]) + dot_last(u_ref[1, f], field_ref[f, 1])
        store_rows(rows_ref, rank_total, value)
        store_slots(starts[f], rows_ref, out_ref, 1, f * cols)
    if cold:
        copies[4].wait()
        copies[5].wait()


def update_kernel(pieces, last, starts_ref, in_ref, v_ref, x_ref, *rest):
    if last:
        new_hbm, rows_ref, left_ref, new_ref, sems = rest
    else:
        new_ref, slots_ref, rows_ref, left_ref, waves_ref = rest
    rank_total, points = v_ref.shape[1:]
    lanes = in_ref.shape[2] // 2
    tiles = in_ref.shape[0]
    starts = [starts_ref[tiles + i, 0] for i in range(tiles // pieces)]
    load_slots(starts, in_ref, rows_ref, pieces, 0)
    real, imag = rows_ref[0, :rank_total, :], rows_ref[1, :rank_total, :]
    left_ref[...] = turned_stack((real, imag), (imag, -real))
    copies = []
    for k, some in enumerate(chunks(points)):
        gradient = dot(left_ref[...], flat(v_ref[:, :, some]))
        real = x_ref[0, some, :] - STEP * gradient[:lanes].T
        imag = x_ref[1, some, :] - STEP * gradient[lanes:].T
        new_ref[0, some, :] = real
        new_ref[1, some, :] = imag
        if last:
            copies.append(
                pltpu.make_async_copy(new_ref.at[:, some, :], new_hbm.at[:, some, :], sems.at[k])
            )
            copies[k].start()
        else:
            waves_ref[0, some, :] = side_by_side(real, imag)
            waves_ref[1, some, :] = side_by_side(-imag, real)
    if last:
        for copy in copies:
            copy.wait()
    else:
        clear_tail(rows_ref, rank_total)
        project(v_ref, waves_ref, rows_ref)
        store_slots(starts, rows_ref, slots_ref, pieces, 0)


def harmonic_sums(freq_count, sample_count):
    multiples = np.arange(2 * freq_count + 1, dtype=np.float64)[:, None]
    phases = 2.0 * math.pi / sample_count * multiples * np.arange(sample_count)[None, :]
    waves = np.stack([np.cos(phases), np.sin(phases)]) / sample_count
    sums = np.concatenate([np.zeros((2, waves.shape[1], 1)), np.cumsum(waves, axis=2)], axis=2)
    return sums.astype(np.float32)


def gram_parts(a, b):
    f, g = a // 2 + 1, b // 2 + 1
    apart, lean = abs(f - g), 1.0 if f > g else -1.0 if f < g else 0.0
    if a % 2 == 0 and b % 2 == 0:
        return [(0, apart, 1.0), (0, f + g, 1.0)]
    if a % 2 == 1 and b % 2 == 1:
        return [(0, apart, 1.0), (0, f + g, -1.0)]
    if a % 2 == 0:
        return [(1, apart, lean), (1, f + g, -1.0)]
    return [(1, apart, -lean), (1, f + g, -1.0)]


def normal_kernel(
    phases, pieces, ranks_ref, start_ref, stop_ref, records_ref, gram_ref, data_ref, starts_ref
):
    @pl.when(pl.program_id(0) == 0)
    def _():
        starts = sum(row_starts(ranks_ref, pieces), []) + column_starts(ranks_ref)
        for k, start in enumerate(starts):
            starts_ref[k, :] = jnp.full(starts_ref.shape[1:], start, jnp.int32)

    parts, samples = phases.shape
    half = samples // 2
    pairs = pair_list(parts)
    sums = harmonic_sums(parts // 2, samples)
    terms = [[term for term in gram_parts(a, b) if term[2] != 0.0] for a, b in pairs]
    needed = sorted({(kind, k) for some in terms for kind, k, _ in some if (kind, k) != (1, 0)})
    chunk = 16

    def pick(level, table, first, last):
        value = jnp.full(level.shape, float(table[first]), F32)
        for t in range(first + 1, last + 1):
            value = jnp.where(level >= t, float(table[t]), value)
        return value

    def add_up(step, carry):
        rows = pl.ds(pl.multiple_of(step * chunk, chunk), chunk)
        begin, end = start_ref[rows, :], stop_ref[rows, :]
        waves = {}
        for kind, k in needed:
            if (kind, k) == (0, 0):
                waves[kind, k] = (end - begin).astype(F32) * (1.0 / samples)
            else:
                table = sums[kind, k]
                waves[kind, k] = pick(end, table, STOP_MIN, STOP_MAX) - pick(
                    begin, table, 0, START_MAX
                )
        for n, some in enumerate(terms):
            total = None
            for kind, k, sign in some:
                if (kind, k) == (1, 0):
                    continue
                if total is None:
                    total = waves[kind, k] if sign > 0 else -waves[kind, k]
                else:
                    total = total + waves[kind, k] if sign > 0 else total - waves[kind, k]
            gram_ref[n, rows, :] = total

        def seen(t):
            value = records_ref[t, rows, :].astype(F32)
            if t < START_MAX:
                value = jnp.where(begin <= t, value, 0.0)
            if t >= STOP_MIN:
                value = jnp.where(end > t, value, 0.0)
            return value

        for odd in (0, 1):
            some = [a for a in range(parts) if (a // 2 + 1) % 2 == odd]
            datas = [jnp.zeros(begin.shape, F32) for _ in some]
            for t in range(half if some else 0):
                late, early = t + half, seen(t)
                if late < STOP_MAX:
                    early = early - seen(late) if odd else early + seen(late)
                for k, a in enumerate(some):
                    datas[k] = datas[k] + float(phases[a, t]) * early
            for k, a in enumerate(some):
                data_ref[a, rows, :] = datas[k]
        return carry

    lax.fori_loop(0, start_ref.shape[0] // chunk, add_up, 0)


def normal_terms(phases, pieces, tile_ranks, window_start, window_stop, records):
    samples, lanes, width = records.shape
    parts = phases.shape[0]
    pair_count = len(pair_list(parts))
    block = 128
    freqs, rows, cols = tile_ranks.shape
    starts = (freqs * cols + rows, block)
    return pl.pallas_call(
        functools.partial(normal_kernel, phases, pieces),
        grid=(width // block,),
        in_specs=[
            SMEM,
            pl.BlockSpec((lanes, block), lambda n: (0, n)),
            pl.BlockSpec((lanes, block), lambda n: (0, n)),
            pl.BlockSpec((samples, lanes, block), lambda n: (0, 0, n)),
        ],
        out_specs=[
            pl.BlockSpec((pair_count, lanes, block), lambda n: (0, 0, n)),
            pl.BlockSpec((parts, lanes, block), lambda n: (0, 0, n)),
            pl.BlockSpec(starts, lambda n: (0, 0)),
        ],
        out_shape=[
            jax.ShapeDtypeStruct((pair_count, lanes, width), F32),
            jax.ShapeDtypeStruct((parts, lanes, width), F32),
            jax.ShapeDtypeStruct(starts, jnp.int32),
        ],
        cost_estimate=pl.CostEstimate(
            flops=16 * records.size, bytes_accessed=3 * records.size, transcendentals=0
        ),
        compiler_params=params(60),
        name="normal_terms",
    )(tile_ranks, window_start, window_stop, records)


def on_device(start_model, v_basis, u_basis, records, tile_ranks, window_start, window_stop):
    tiles = lax.axis_size("tile")
    freqs, rows, cols = tile_ranks.shape
    pieces = tiles // rows
    rank_total = v_basis.shape[1]
    points, lanes = start_model.shape[1:]
    receivers = u_basis.shape[3]
    phases = phase_rows(freqs, records.shape[0])

    slots = jax.ShapeDtypeStruct((tiles, RMAX, 2 * lanes), BF16)
    model = jax.ShapeDtypeStruct(start_model.shape, F32)
    v_like = jax.ShapeDtypeStruct(v_basis.shape, BF16)
    padded_rows = pltpu.VMEM((2, rank_total + RMAX, lanes), F32)
    waves = pltpu.VMEM((2, points, 2 * lanes), BF16)
    left = pltpu.VMEM((2 * lanes, 2 * rank_total), BF16)
    exchange = lambda x: lax.all_to_all(x, "tile", split_axis=0, concat_axis=0, tiled=True)

    outgoing = pl.pallas_call(
        functools.partial(first_kernel, pieces),
        in_specs=[HBM, HBM, HBM],
        out_specs=HBM,
        out_shape=slots,
        scratch_shapes=[
            pltpu.SMEM(tile_ranks.shape, tile_ranks.dtype),
            pltpu.VMEM(v_basis.shape, BF16),
            pltpu.VMEM(start_model.shape, F32),
            waves,
            padded_rows,
            pltpu.VMEM(slots.shape, BF16),
            pltpu.SemaphoreType.DMA((3,)),
            pltpu.SemaphoreType.DMA((2,)),
        ],
        compiler_params=params(60),
        name="first_projection",
    )(tile_ranks, v_basis, start_model)
    *normal, starts = normal_terms(
        phases, pieces, tile_ranks, window_start, window_stop, records
    )
    in_hbm = lambda x: pltpu.with_memory_space_constraint(x, pltpu.HBM)
    fetch = [
        pltpu.SMEM(tile_ranks.shape, tile_ranks.dtype),
        pltpu.VMEM(slots.shape, BF16),
        *[pltpu.VMEM(x.shape, F32) for x in normal],
        pltpu.VMEM((freqs, 2 * lanes, receivers), F32),
        pltpu.SemaphoreType.DMA((6,)),
    ]
    finish = [
        pltpu.VMEM(start_model.shape, F32),
        pltpu.SemaphoreType.DMA((len(chunks(points)),)),
    ]
    current = start_model
    for iteration in range(ITERS):
        cold = iteration == 0
        terms = [in_hbm(x) for x in normal] if cold else normal
        early = [in_hbm(v_basis), in_hbm(current)] if cold else []
        arrived = exchange(outgoing)
        result = pl.pallas_call(
            functools.partial(misfit_kernel, pieces, cold),
            in_specs=[HBM, HBM, VMEM, HBM, HBM, HBM, HBM] if cold else [VMEM] * 5,
            out_specs=[VMEM] * 3 if cold else VMEM,
            out_shape=[slots, v_like, model] if cold else slots,
            scratch_shapes=[
                padded_rows,
                pltpu.VMEM((freqs, 2 * lanes, 2 * rank_total), BF16),
                pltpu.VMEM((freqs, 2, 2 * lanes, receivers), BF16),
            ]
            + (fetch if cold else []),
            compiler_params=params(8 + mebibytes(slots, v_basis, model, *normal)),
            name="misfit",
        )(tile_ranks if cold else starts, arrived, u_basis, *terms, *early)
        if cold:
            outgoing, v_basis, current = result
        else:
            outgoing = result
        arrived = exchange(outgoing)
        last = iteration == ITERS - 1
        result = pl.pallas_call(
            functools.partial(update_kernel, pieces, last),
            in_specs=[VMEM] * 4,
            out_specs=HBM if last else [VMEM, VMEM],
            out_shape=model if last else [model, slots],
            scratch_shapes=[padded_rows, left] + (finish if last else [waves]),
            compiler_params=params(12),
            name="last_update" if last else "update",
        )(starts, arrived, v_basis, current)
        if last:
            current = result
        else:
            current, outgoing = result
    return current


def solution(mesh):
    in_specs = (
        P(None, ("groups", "tile"), None),
        P(None, ("groups", "tile"), None),
        P(None, None, None, ("groups", "tile")),
        P(None, None, ("groups", "tile")),
        P("groups", None, None),
        P(None, ("groups", "tile")),
        P(None, ("groups", "tile")),
    )
    out_specs = P(None, ("groups", "tile"), None)
    return jax.shard_map(
        on_device, mesh=mesh, in_specs=in_specs, out_specs=out_specs, check_vma=False
    )
```
